256 devices in a mesh: dp: 32 (over y, x, z_lo), seq: 8 (over z_hi, core).
Axes of the slice: x: 4, y: 4, z: 8 (z_hi: 4, z_lo: 2; z = z_hi * 2 + z_lo), core: 2. Of those that a mesh axis runs over, the one named last changes fastest.
Arguments:
- queries: bfloat16 [32, 1024, 1536], P('dp', 'seq'), may hold values from -6 to 6
- key_states: bfloat16 [32, 1024, 1536], P('dp', 'seq'), may hold values from -6 to 6
- value_states: bfloat16 [32, 1024, 1536], P('dp', 'seq'), may hold values from -6 to 6
- segment_ids: int32 [32, 1024], P('dp'), may hold values from 0 to 2, never falling along the last dimension, each value on 1 to 512 neighbouring positions
- inner_first: bfloat16 [24, 64, 256], replicated, may hold values from -0.75 to 0.75
- inner_second: bfloat16 [24, 64, 256], replicated, may hold values from -0.375 to 0.375
- inner_rate: float32 [24], replicated, may hold values from 0.02 to 0.3
- branch_gate: float32 [1536], replicated, may hold values from -1.5 to 1.5
- out_weight: bfloat16 [1536, 3072], P('dp'), may hold values from -0.15625 to 0.15625
Outputs:
- layer_out: bfloat16 [32, 1024, 3072], P('dp', 'seq')
The draws below stay inside these ranges and needn't reach their ends.
Inputs may be any that keep to these rules, and one draw needn't show every extreme that they name: `segment_ids`: segment numbers never fall along a clip; each segment holds 1 to 512 tokens and one holds exactly 512.
All inputs are finite; a program needn't handle non-finite values.
Results may differ from the reference program's by a relative error of at most 0.006.
Values may be sent and summed in bfloat16 or wider, within the bound.
No kernel may reach another device: no remote copies, remote signals or barrier semaphores. Data moves between devices by JAX's collectives and lax.ppermute only.
A program may use at most 64 MiB of HBM per device.

```python
import math
import jax
import jax.numpy as jnp
import numpy as np
from jax import lax

D = 3072
HD = 64
HEADS = 24
FFI = 256
CH = 64
SEG_COUNT = 3
TOK_DEV = 128
CLIPS = 32
LEN = 1024
HH = 1536
SEG_MOST = 512


def draw_queries(key, part):
    key = jax.random.fold_in(key, 1)
    result = jnp.clip(jax.random.normal(key, (CLIPS, LEN, HH), jnp.float32), -6.0, 6.0)
    return result.astype(jnp.bfloat16)


def draw_key_states(key, part):
    key = jax.random.fold_in(key, 2)
    result = jnp.clip(jax.random.normal(key, (CLIPS, LEN, HH), jnp.float32), -6.0, 6.0)
    return result.astype(jnp.bfloat16)


def shard_levels(key, extent, pieces, smallest, largest):
    level, own = 1.0, jax.random.fold_in(key, 6)
    for dim, parts in pieces:
        draws = jnp.exp(jax.random.uniform(jax.random.fold_in(own, dim), (parts,), jnp.float32, smallest / len(pieces), largest / len(pieces)))
        level = level * jnp.repeat(draws, extent[dim] // parts).reshape([-1 if axis == dim else 1 for axis in range(len(extent))])
    return level


def split_up(amount, total, reach, skew):
    weights = [(1 << 20) // math.isqrt(standing ** skew) + 1 for standing in range(2, amount + 1)]
    spare, given = total - reach - (amount - 1), [1] * (amount - 1)
    while spare > 0:
        movable = [i for i in range(amount - 1) if given[i] < reach]
        mass, budget = sum([weights[i] for i in movable]), spare
        for i in movable:
            addition = min(reach - given[i], max(1, budget * weights[i] // mass), spare)
            given[i] = given[i] + addition
            spare = spare - addition
    return np.array([reach] + given)


def ragged_sizes(rng, amount, total, most, slope):
    if amount == 2:
        one = jax.random.randint(rng, (), max(1, total - most), min(most, total - 1) + 1)
        return jnp.stack([one, total - one])
    tallies = jnp.asarray(split_up(amount, total, most, slope), jnp.int32)
    pairs = (amount - 1) // 2
    donor, receiver = tallies[1:1 + 2 * pairs:2], tallies[2:2 + 2 * pairs:2]
    slack = jnp.minimum(donor - 1, most - receiver)
    moved = jax.random.randint(jax.random.fold_in(rng, 1), (pairs,), 0, 1 << 20) % (slack + 1)
    tallies = tallies.at[1:1 + 2 * pairs:2].set(donor - moved).at[2:2 + 2 * pairs:2].set(receiver + moved)
    return tallies[jax.random.permutation(jax.random.fold_in(rng, 2), amount)]


def normal_values(own_key, dims, scale, reach, cuts=(), held_as=jnp.bfloat16):
    gain = shard_levels(own_key, dims, cuts, -0.22, 0.18) if cuts else 1.0
    entries = jax.random.normal(own_key, dims, jnp.float32) * scale * gain
    return jnp.minimum(jnp.maximum(entries, -reach), reach).astype(held_as)


def setup_inputs(seed: int = 0) -> dict:
    seeds = jax.random.split(jax.random.key(seed), 10)
    return {
        "queries": draw_queries(jax.random.fold_in(seeds[9], 71), 0),
        "key_states": draw_key_states(jax.random.fold_in(seeds[9], 71), 0),
        "value_states": normal_values(seeds[2], (CLIPS, LEN, HH), 1.0, 6.0, ((0, 32), (1, 8))),
        "segment_ids": jax.vmap(lambda own: jnp.searchsorted(jnp.cumsum(ragged_sizes(own, SEG_COUNT, LEN, SEG_MOST, 1)), jnp.arange(LEN), side="right"))(jax.random.split(seeds[3], CLIPS)).reshape((CLIPS, LEN)).astype(jnp.int32),
        "inner_first": normal_values(seeds[4], (HEADS, HD, FFI), HD ** -0.5, 0.75),
        "inner_second": normal_values(seeds[5], (HEADS, HD, FFI), FFI ** -0.5, 0.375),
        "inner_rate": jnp.clip(jnp.exp(jax.random.uniform(seeds[6], (HEADS,), jnp.float32, math.log(0.02), math.log(0.3))), 0.02, 0.3),
        "branch_gate": jnp.clip(jax.random.uniform(seeds[7], (HH,), jnp.float32, -1.5, 1.5), -1.5, 1.5),
        "out_weight": normal_values(seeds[8], (HH, D), HH ** -0.5, 0.15625, ((0, 32),)),
    }


def dense(form, left, right):
    return jnp.einsum(form, left, right, precision=lax.Precision.HIGHEST)

def inner_norm(matrix):
    center = matrix - lax.optimization_barrier(jnp.mean(matrix, axis=-1, keepdims=True))
    spread = lax.optimization_barrier(jnp.mean(center * center, axis=-1, keepdims=True))
    return center / jnp.sqrt(spread + 1e-06)

def rms_scale(matrix):
    return matrix / jnp.sqrt(lax.optimization_barrier(jnp.mean(matrix * matrix, axis=-1, keepdims=True)) + 1e-06)

def pack(weight_in, weight_out, bias_in, bias_out):
    width = weight_in.shape[1]
    hidden = weight_in.shape[2]
    padded = jnp.pad(bias_out, ((0, 0), (0, hidden - width)))
    return jnp.concatenate([weight_in, weight_out, bias_in[:, None, :], padded[:, None, :]], axis=1)

def unpack(state):
    width = (state.shape[1] - 2) // 2
    return (state[:, :width], state[:, width:2 * width], state[:, 2 * width], state[:, 2 * width + 1, :width])

def inner_span(carry, block, step_rate):
    weight_in, weight_out, bias_in, bias_out = carry
    query_part, key_part, value_part = block
    rate = step_rate[:, None, None]
    length = query_part.shape[1]
    hidden_pre = dense('hcd,hdf->hcf', key_part, weight_in) + bias_in[:, None, :]
    hidden_act, gelu_back = jax.vjp(jax.nn.gelu, hidden_pre)
    out_pre = dense('hcf,hdf->hcd', hidden_act, weight_out) + bias_out[:, None, :]
    normed, norm_back = jax.vjp(inner_norm, out_pre)
    error = normed - (value_part - key_part)
    grad_out = norm_back(error)[0]
    grad_hidden = gelu_back(dense('hcd,hdf->hcf', grad_out, weight_out))[0]
    causal = jnp.tril(jnp.ones((length, length), jnp.float32))
    first_kernel = (dense('hcd,hsd->hcs', query_part, key_part) + 1.0) * causal
    query_pre = dense('hcd,hdf->hcf', query_part, weight_in) + bias_in[:, None, :] - rate * dense('hcs,hsf->hcf', first_kernel, grad_hidden)
    query_act = jax.nn.gelu(query_pre)
    second_kernel = (dense('hcf,hsf->hcs', query_act, hidden_act) + 1.0) * causal
    query_out = dense('hcf,hdf->hcd', query_act, weight_out) + bias_out[:, None, :] - rate * dense('hcs,hsd->hcd', second_kernel, grad_out)
    result = query_part + inner_norm(query_out)
    new_in = weight_in - rate * dense('hsd,hsf->hdf', key_part, grad_hidden)
    new_bias_in = bias_in - step_rate[:, None] * lax.optimization_barrier(jnp.sum(grad_hidden, axis=1))
    new_out = weight_out - rate * dense('hsd,hsf->hdf', grad_out, hidden_act)
    new_bias_out = bias_out - step_rate[:, None] * lax.optimization_barrier(jnp.sum(grad_out, axis=1))
    return ((new_in, new_out, new_bias_in, new_bias_out), result)

def inner_run(query_part, key_part, value_part, state, step_rate):
    heads, length, width = query_part.shape
    blocks = length // CH

    def split(array):
        return array.reshape(heads, blocks, CH, width).transpose(1, 0, 2, 3)

    def advance(carry, block):
        return inner_span(carry, block, step_rate)
    final, outputs = lax.scan(advance, unpack(state), (split(query_part), split(key_part), split(value_part)))
    return (outputs.transpose(1, 0, 2, 3).reshape(heads, length, width), pack(*final))

def prepare(query_rows, key_rows, value_rows):
    count = query_rows.shape[0]
    heads = query_rows.shape[1] // HD

    def heads_first(rows):
        return rows.reshape(count, heads, HD).transpose(1, 0, 2).astype(jnp.float32)
    return (rms_scale(heads_first(query_rows)), rms_scale(heads_first(key_rows)), heads_first(value_rows))

def attend_clip(query_rows, key_rows, value_rows, segment_row):
    blocks = LEN // TOK_DEV

    def heads_first(rows):
        return rows.reshape(LEN, HEADS, HD).transpose(1, 0, 2).astype(jnp.float32)

    def one_head(arrays):
        query_head, key_head, value_head = arrays

        def one_block(index):
            begin = (index * TOK_DEV).astype(jnp.int32)
            query_block = lax.dynamic_slice_in_dim(query_head, begin, TOK_DEV, 0)
            query_seg = lax.dynamic_slice_in_dim(segment_row, begin, TOK_DEV, 0)
            allowed = query_seg[:, None] == segment_row[None, :]
            scores = jnp.einsum('qd,kd->qk', query_block, key_head) * HD ** (-0.5)
            scores = jnp.where(allowed, scores, -1e+30)
            top = lax.optimization_barrier(jnp.max(scores, axis=-1, keepdims=True))
            expo = jnp.where(allowed, jnp.exp(scores - top), 0.0)
            total = lax.optimization_barrier(jnp.sum(expo, axis=-1, keepdims=True))
            shares = expo.astype(jnp.bfloat16).astype(jnp.float32)
            return jnp.einsum('qk,kd->qd', shares, value_head) / total
        return lax.map(one_block, jnp.arange(blocks, dtype=jnp.int32)).reshape(LEN, HD)
    return lax.map(one_head, (heads_first(query_rows), heads_first(key_rows), heads_first(value_rows)))

def combine(attended, inner_out, branch_gate):
    heads, count, width = attended.shape
    joined = attended.transpose(1, 0, 2).reshape(count, heads * width)
    inner_rows = inner_out.transpose(1, 0, 2).reshape(count, heads * width)
    return (joined + jnp.tanh(branch_gate)[None, :] * inner_rows).astype(jnp.bfloat16)

def reference(queries, key_states, value_states, segment_ids, inner_first, inner_second, inner_rate, branch_gate, out_weight):
    heads = inner_first.shape[0]
    start_state = pack(inner_first.astype(jnp.float32), inner_second.astype(jnp.float32), jnp.zeros((heads, FFI), jnp.float32), jnp.zeros((heads, HD), jnp.float32))
    step_rate = inner_rate / HD

    def one_clip(clip):
        query_rows, key_rows, value_rows, segment_row = clip
        attended = attend_clip(query_rows, key_rows, value_rows, segment_row)
        query_part, key_part, value_part = prepare(query_rows, key_rows, value_rows)
        inner_out, final_state = inner_run(query_part, key_part, value_part, start_state, step_rate)
        mixed = combine(attended, inner_out, branch_gate)
        return jnp.dot(mixed, out_weight, preferred_element_type=jnp.float32).astype(jnp.bfloat16)
    return lax.map(one_clip, (queries, key_states, value_states, segment_ids))
```

```python
import functools
import math

import jax
import jax.numpy as jnp
from jax import lax
from jax.experimental import pallas as pl
from jax.experimental.pallas import tpu as pltpu
from jax.sharding import PartitionSpec as P

HD = 64
FFI = 256
CH = 64
LOCAL = 3
PARTS = 8
TOK = 128
LEN = 1024
HH = 1536
WIDTH = LOCAL * HD
SAME = 32.0
EPS = 1e-6
GA = math.sqrt(2.0 / math.pi)
GB = GA * 0.044715
VMEM_MOST = 56 * 1024 * 1024

f32 = jnp.float32
bf16 = jnp.bfloat16


def dot(left, right):
    return jnp.dot(left, right, preferred_element_type=f32)


def dot_nt(left, right):
    return lax.dot_general(left, right, (((1,), (1,)), ((), ())), preferred_element_type=f32)


def dot_tn(left, right):
    return lax.dot_general(left, right, (((0,), (0,)), ((), ())), preferred_element_type=f32)


def lane_mean(value):
    return jnp.mean(value, axis=-1, keepdims=True)


def pack_kernel(me_ref, q_ref, k_ref, v_ref, *rest):
    outs, held, sems = rest[:PARTS], rest[PARTS], rest[PARTS + 1]
    for part in range(PARTS):
        cols = slice(part * WIDTH, (part + 1) * WIDTH)
        for group, ref in enumerate((q_ref, k_ref, v_ref)):
            for half in range(2):
                at = (2 * group + half) * WIDTH
                held[part, :, at : at + WIDTH] = ref[half * CH : (half + 1) * CH, cols]
    me = me_ref[0]
    copies = []
    for step in range(PARTS):
        copies.append(pltpu.make_async_copy(held.at[lax.rem(me + step, PARTS)], outs[step], sems.at[step]))
    for copy in copies:
        copy.start()
    for copy in copies:
        copy.wait()


def pack(me, queries, keys, values):
    vmem = pl.BlockSpec(memory_space=pltpu.VMEM)
    return pl.pallas_call(
        pack_kernel,
        out_shape=[jax.ShapeDtypeStruct((CH, 6 * WIDTH), bf16)] * PARTS,
        in_specs=[pl.BlockSpec(memory_space=pltpu.SMEM), vmem, vmem, vmem],
        out_specs=[pl.BlockSpec(memory_space=pl.ANY)] * PARTS,
        scratch_shapes=[pltpu.VMEM((PARTS, CH, 6 * WIDTH), bf16), pltpu.SemaphoreType.DMA((PARTS,))],
        compiler_params=pltpu.CompilerParams(vmem_limit_bytes=VMEM_MOST),
        name="pack_rows",
    )(me, queries, keys, values)


def gelu_parts(z, slope):
    square = z * z
    half = 0.5 * jnp.tanh(z * (GB * square + GA)) + 0.5
    act = z * half
    if not slope:
        return act, None
    return act, half + (act - act * half) * (6.0 * GB * square + 2.0 * GA)


def heads_kernel(
    me_ref, rate_ref, *rest,
):
    xs = rest[:PARTS]
    seg_ref, first_ref, second_ref, gate_ref = rest[PARTS : PARTS + 4]
    outs = rest[PARTS + 4 : 2 * PARTS + 4]
    (
        x, w1, w2, mixed, q_aug, k_aug, v_aug, att,
        w1s, w2s, b1s, b2s, z1s, q1s, a_prev, g2_prev, b2_prev, xq_prev,
        sems, wsems,
    ) = rest[2 * PARTS + 4 :]
    me = me_ref[0]
    copies = [
        pltpu.make_async_copy(xs[step], x.at[lax.rem(me + PARTS - step, PARTS)], sems.at[step])
        for step in range(PARTS)
    ]
    weights = [
        pltpu.make_async_copy(first_ref.at[pl.ds(me * LOCAL, LOCAL)], w1, wsems.at[0]),
        pltpu.make_async_copy(second_ref.at[pl.ds(me * LOCAL, LOCAL)], w2, wsems.at[1]),
    ]
    for copy in copies + weights:
        copy.start()
    for copy in copies + weights:
        copy.wait()

    def cut(group, head, source, half):
        at = (2 * group + half) * WIDTH + head * HD
        return x[source, :, at : at + HD]

    def prepare(source, carry):
        for half in range(2):
            rows = pl.ds(pl.multiple_of(source * TOK + half * CH, CH), CH)
            seg = seg_ref[rows, :]
            ones = jnp.ones((CH, HD), bf16)
            for head in range(LOCAL):
                q_aug[head, rows, :] = jnp.concatenate([cut(0, head, source, half) * 0.125, seg], axis=1).astype(bf16)
                k_aug[head, rows, :] = jnp.concatenate([cut(1, head, source, half), seg], axis=1)
                v_aug[head, rows, :] = jnp.concatenate([cut(2, head, source, half), ones], axis=1)
        return carry

    lax.fori_loop(0, PARTS, prepare, 0)

    def attend(source, carry):
        rows = pl.ds(pl.multiple_of(source * TOK, TOK), TOK)
        for head in range(LOCAL):
            scores = dot_nt(q_aug[head, rows, :], k_aug[head])
            top = jnp.max(scores, axis=-1, keepdims=True)
            shares = jnp.exp(scores - top).astype(bf16)
            got = dot(shares, v_aug[head])
            att[head, rows, :] = got[:, :HD] / got[:, HD:]
        return carry

    lax.fori_loop(0, PARTS, attend, 0)

    causal = lax.broadcasted_iota(jnp.int32, (CH, CH), 0) >= lax.broadcasted_iota(jnp.int32, (CH, CH), 1)

    def rms(value):
        return lax.rsqrt(lane_mean(value * value) + EPS)

    def stacked(head, q_source, q_half, k_source, k_half):
        q = cut(0, head, q_source, q_half)
        k = cut(1, head, k_source, k_half)
        rows = jnp.concatenate([q, k], axis=0)
        wide = rows.astype(f32)
        scale = rms(wide)
        return rows, wide * scale, scale

    def project(head, rows, scale):
        state = w1s[head]
        high = state.astype(bf16)
        low = (state - high.astype(f32)).astype(bf16)
        both = dot(jnp.concatenate([rows, rows], axis=1), jnp.concatenate([high, low], axis=0))
        return both * scale + b1s[head]

    for head in range(LOCAL):
        w1s[head] = w1[head].astype(f32)
        start = w2[head].astype(f32)
        w2s[head] = start - jnp.mean(start, axis=0, keepdims=True)
        b1s[head] = jnp.zeros((1, FFI), f32)
        b2s[head] = jnp.zeros((1, HD), f32)
        b2_prev[head] = jnp.zeros((1, HD), f32)
        k = cut(1, head, 0, 0)
        z1s[head] = project(head, k, rms(k.astype(f32)))
        q1s[head] = jnp.zeros((CH, FFI), f32)
        a_prev[head] = jnp.zeros((CH + HD, FFI), bf16)
        g2_prev[head] = jnp.zeros((CH, HD), bf16)
        xq_prev[head] = jnp.zeros((CH, HD), f32)

    def query_side(block):
        rows = pl.ds(pl.multiple_of(block * CH, CH), CH)
        for head in range(LOCAL):
            act, _ = gelu_parts(q1s[head], False)
            high = act.astype(bf16)
            low = (act - high.astype(f32)).astype(bf16)
            both = dot_nt(high, a_prev[head])
            second = jnp.where(causal, both[:, :CH] + 1.0, 0.0).astype(bf16)
            out = both[:, CH:] + dot_nt(low, a_prev[head, CH:, :]) + b2_prev[head] - dot(second, g2_prev[head])
            inner = xq_prev[head] + out * lax.rsqrt(lane_mean(out * out) + EPS)
            gate = jnp.tanh(gate_ref[me * LOCAL + head])
            yield (att[head, rows, :] + gate * inner).astype(bf16)

    def key_side(source, half, next_source, next_half):
        for head in range(LOCAL):
            eta = rate_ref[me * LOCAL + head] * (1.0 / HD)
            k = cut(1, head, source, half).astype(f32)
            keys = k * rms(k)
            target = cut(2, head, source, half).astype(f32) - keys
            target = target - lane_mean(target)
            keys_low = keys.astype(bf16)
            rows, normed, scale = stacked(head, source, half, next_source, next_half)
            ahead = project(head, rows, scale)
            cross = dot_nt(normed.astype(bf16), keys_low) + 1.0
            cross = jnp.concatenate([jnp.where(causal, cross[:CH], 0.0), cross[CH:]], axis=0).astype(bf16)

            act, slope = gelu_parts(z1s[head], True)
            act_low = act.astype(bf16)
            second = w2s[head]
            second_low = second.astype(bf16)
            c = dot_nt(act_low, second_low) + b2s[head]
            r = lax.rsqrt(lane_mean(c * c) + EPS)
            mix = lane_mean(c * target)
            grad = (eta * r) * (c * (r * (EPS * r * r + mix * r)) - target)
            grad_low = grad.astype(bf16)
            deep = dot(grad_low, second_low) * slope
            deep_low = deep.astype(bf16)
            both = ahead - dot(cross, deep_low)

            q1s[head] = both[:CH]
            z1s[head] = both[CH:]
            a_prev[head, :CH, :] = act_low
            a_prev[head, CH:, :] = second_low
            g2_prev[head] = grad_low
            b2_prev[head] = b2s[head]
            xq_prev[head] = normed[:CH]
            w1s[head] = w1s[head] - dot_tn(keys_low, deep_low)
            b1s[head] = b1s[head] - jnp.sum(deep, axis=0, keepdims=True)
            w2s[head] = second - dot_tn(grad_low, act_low)
            b2s[head] = b2s[head] - jnp.sum(grad, axis=0, keepdims=True)

    def blocks(source, carry):
        for head, rows in enumerate(query_side(jnp.maximum(2 * source - 1, 0))):
            mixed[source, :, WIDTH + head * HD : WIDTH + (head + 1) * HD] = rows
        key_side(source, 0, source, 1)
        for head, rows in enumerate(query_side(2 * source)):
            mixed[source + 1, :, head * HD : (head + 1) * HD] = rows
        key_side(source, 1, jnp.minimum(source + 1, PARTS - 1), 0)
        return carry

    lax.fori_loop(0, PARTS, blocks, 0)
    for head, rows in enumerate(query_side(2 * PARTS - 1)):
        mixed[PARTS, :, WIDTH + head * HD : WIDTH + (head + 1) * HD] = rows

    copies = [
        pltpu.make_async_copy(mixed.at[1 + lax.rem(me + step, PARTS)], outs[step], sems.at[step])
        for step in range(PARTS)
    ]
    for copy in copies:
        copy.start()
    for copy in copies:
        copy.wait()


def run_heads(me, rate, pieces, seg, first, second, gate):
    vmem = pl.BlockSpec(memory_space=pltpu.VMEM)
    smem = pl.BlockSpec(memory_space=pltpu.SMEM)
    hbm = pl.BlockSpec(memory_space=pl.ANY)
    return pl.pallas_call(
        heads_kernel,
        out_shape=[jax.ShapeDtypeStruct((CH, 2 * WIDTH), bf16)] * PARTS,
        in_specs=[smem, smem] + [hbm] * PARTS + [vmem, hbm, hbm, vmem],
        out_specs=[hbm] * PARTS,
        scratch_shapes=[
            pltpu.VMEM((PARTS, CH, 6 * WIDTH), bf16),
            pltpu.VMEM((LOCAL, HD, FFI), bf16),
            pltpu.VMEM((LOCAL, HD, FFI), bf16),
            pltpu.VMEM((PARTS + 1, CH, 2 * WIDTH), bf16),
            pltpu.VMEM((LOCAL, LEN, 2 * HD), bf16),
            pltpu.VMEM((LOCAL, LEN, 2 * HD), bf16),
            pltpu.VMEM((LOCAL, LEN, 2 * HD), bf16),
            pltpu.VMEM((LOCAL, LEN, HD), f32),
            pltpu.VMEM((LOCAL, HD, FFI), f32),
            pltpu.VMEM((LOCAL, HD, FFI), f32),
            pltpu.VMEM((LOCAL, 1, FFI), f32),
            pltpu.VMEM((LOCAL, 1, HD), f32),
            pltpu.VMEM((LOCAL, CH, FFI), f32),
            pltpu.VMEM((LOCAL, CH, FFI), f32),
            pltpu.VMEM((LOCAL, CH + HD, FFI), bf16),
            pltpu.VMEM((LOCAL, CH, HD), bf16),
            pltpu.VMEM((LOCAL, 1, HD), f32),
            pltpu.VMEM((LOCAL, CH, HD), f32),
            pltpu.SemaphoreType.DMA((PARTS,)),
            pltpu.SemaphoreType.DMA((2,)),
        ],
        compiler_params=pltpu.CompilerParams(vmem_limit_bytes=VMEM_MOST),
        name="run_heads",
    )(me, rate, *pieces, seg, first, second, gate)


def project_kernel(place_ref, *rest):
    mixed = rest[:PARTS]
    own, sib = rest[PARTS : PARTS + 4], rest[PARTS + 4 : PARTS + 8]
    out, held, weight, sems, wsems = rest[PARTS + 8 :]
    me, dp = place_ref[0], place_ref[1]
    core = lax.rem(me, 2)
    copies = [
        pltpu.make_async_copy(mixed[step], held.at[lax.rem(me + PARTS - step, PARTS)], sems.at[step])
        for step in range(PARTS)
    ]
    y, x, z = dp // 8, lax.rem(dp // 2, 4), lax.rem(dp, 2)
    for side, blocks in enumerate((own, sib)):
        axis = core if side == 0 else 1 - core
        for i, far in enumerate(STEPS):
            for j, near in enumerate(STEPS):
                dx = jnp.where(axis == 0, near, far)
                dy = jnp.where(axis == 0, far, near)
                line = lax.rem(y + 4 - dy, 4) * 8 + lax.rem(x + 4 - dx, 4) * 2
                for flip in range(2):
                    row = pl.multiple_of((line + (z + flip) - 2 * z * flip) * ROWS, ROWS)
                    slot = (2 * j + flip) * ROWS
                    copies.append(
                        pltpu.make_async_copy(
                            blocks[i].at[pl.ds(slot, ROWS)],
                            weight.at[axis, pl.ds(row, ROWS)],
                            wsems.at[side, 8 * i + 2 * j + flip],
                        )
                    )
    for copy in copies:
        copy.start()
    for copy in copies:
        copy.wait()
    rows = [jnp.concatenate([held[part, :, half * WIDTH : (half + 1) * WIDTH] for part in range(PARTS)], axis=1) for half in range(2)]
    rows = jnp.concatenate(rows, axis=0)
    wide = weight.shape[2]
    for side in range(2):
        for at in range(0, wide, 256):
            out[:, side * wide + at : side * wide + at + 256] = dot(rows, weight[side, :, at : at + 256]).astype(bf16)


def run_project(place, mixed, own, sib):
    hbm = pl.BlockSpec(memory_space=pl.ANY)
    wide = own[0].shape[1]
    return pl.pallas_call(
        project_kernel,
        out_shape=jax.ShapeDtypeStruct((TOK, 2 * wide), bf16),
        in_specs=[pl.BlockSpec(memory_space=pltpu.SMEM)] + [hbm] * (PARTS + 8),
        out_specs=pl.BlockSpec(memory_space=pltpu.VMEM),
        scratch_shapes=[
            pltpu.VMEM((PARTS, CH, 2 * WIDTH), bf16),
            pltpu.VMEM((2, HH, wide), bf16),
            pltpu.SemaphoreType.DMA((PARTS,)),
            pltpu.SemaphoreType.DMA((2, 32)),
        ],
        compiler_params=pltpu.CompilerParams(vmem_limit_bytes=VMEM_MOST),
        name="project_rows",
    )(place, *mixed, *own, *sib)


ROWS = HH // 32
STEPS = (0, 1, 3, 2)


def where_is(index):
    dp, seq = divmod(index, PARTS)
    return dp // 8, (dp // 2) % 4, dp % 2, seq // 2, seq % 2


def index_of(y, x, z, group, core):
    return ((y % 4) * 8 + (x % 4) * 2 + z % 2) * PARTS + (group % 4) * 2 + core % 2


def move(array, place):
    pairs = [(i, index_of(*place(*where_is(i)))) for i in range(32 * PARTS)]
    return lax.ppermute(array, ("dp", "seq"), pairs)


def turn(array, step):
    return lax.ppermute(array, "seq", [(i, (i + step) % PARTS) for i in range(PARTS)])


def near_axis(step):
    return lambda y, x, z, group, core: (y + step * core, x + step * (1 - core), z, group, core)


def far_axis(step):
    return lambda y, x, z, group, core: (y + step * (1 - core), x + step * core, z, group, core)


def flip_z(y, x, z, group, core):
    return y, x, 1 - z, group, core


def flip_core(y, x, z, group, core):
    return y, x, z, group, 1 - core


def on_device(
    queries, key_states, value_states, segment_ids, inner_first, inner_second, inner_rate, branch_gate, out_weight
):
    seq, dp = lax.axis_index("seq"), lax.axis_index("dp")
    place = jnp.stack([seq, dp]).astype(jnp.int32)
    wide = out_weight.shape[1] // 2
    slab = lax.dynamic_slice_in_dim(out_weight, (seq % 2) * wide, wide, 1)
    slab = jnp.concatenate([slab, move(slab, flip_z)], axis=0)

    pieces = pack(place, queries[0], key_states[0], value_states[0])
    pieces = [pieces[0]] + [turn(pieces[step], step) for step in range(1, PARTS)]

    slab = jnp.concatenate([slab] + [move(slab, near_axis(step)) for step in STEPS[1:]], axis=0)
    own = [slab] + [move(slab, far_axis(step)) for step in STEPS[1:]]

    seg = jnp.where(segment_ids[0][:, None] == jnp.arange(HD)[None, :], SAME, 0.0).astype(bf16)
    gate = branch_gate.reshape(-1, 1, HD)
    mixed = run_heads(place, inner_rate, pieces, seg, inner_first, inner_second, gate)
    mixed = [mixed[0]] + [turn(mixed[step], step) for step in range(1, PARTS)]
    sib = [move(block, flip_core) for block in own]
    return run_project(place, mixed, own, sib)[None]


def solution(mesh):
    in_specs = (
        P("dp", "seq", None),
        P("dp", "seq", None),
        P("dp", "seq", None),
        P("dp", None),
        P(),
        P(),
        P(),
        P(),
        P("dp", None),
    )
    return jax.shard_map(
        on_device, mesh=mesh, in_specs=in_specs, out_specs=P("dp", "seq", None), check_vma=False
    )
```

```python
import functools
import math

import jax
import jax.numpy as jnp
from jax import lax
from jax.experimental import pallas as pl
from jax.experimental.pallas import tpu as pltpu
from jax.sharding import PartitionSpec as P

HD = 64
FFI = 256
CH = 64
LOCAL = 3
PARTS = 8
TOK = 128
LEN = 1024
HH = 1536
WIDTH = LOCAL * HD
SAME = 32.0
EPS = 1e-6
GA = math.sqrt(2.0 / math.pi)
GB = GA * 0.044715
VMEM_MOST = 56 * 1024 * 1024

f32 = jnp.float32
bf16 = jnp.bfloat16


def dot(left, right):
    return jnp.dot(left, right, preferred_element_type=f32)


def dot_nt(left, right):
    return lax.dot_general(left, right, (((1,), (1,)), ((), ())), preferred_element_type=f32)


def dot_tn(left, right):
    return lax.dot_general(left, right, (((0,), (0,)), ((), ())), preferred_element_type=f32)


def lane_mean(value):
    return jnp.mean(value, axis=-1, keepdims=True)


MOVES = ((2, 0), (1, 0), (3, 0), (2, 1), (1, 1), (3, 1), (0, 1))


def target_of(me, step):
    chips, swap = MOVES[step - 1] if step else (0, 0)
    core = lax.rem(me, 2)
    return lax.rem(me // 2 + chips, 4) * 2 + (1 - core if swap else core)


def source_of(me, step):
    chips, swap = MOVES[step - 1] if step else (0, 0)
    core = lax.rem(me, 2)
    return lax.rem(me // 2 + 4 - chips, 4) * 2 + (1 - core if swap else core)


def pack_kernel(q_ref, k_ref, v_ref, out):
    for part in range(PARTS):
        cols = slice(part * WIDTH, (part + 1) * WIDTH)
        for group, ref in enumerate((q_ref, k_ref, v_ref)):
            for half in range(2):
                at = (2 * group + half) * WIDTH
                out[part, :, at : at + WIDTH] = ref[half * CH : (half + 1) * CH, cols]


def pack(queries, keys, values):
    return pl.pallas_call(
        pack_kernel,
        out_shape=jax.ShapeDtypeStruct((PARTS, CH, 6 * WIDTH), bf16),
        compiler_params=pltpu.CompilerParams(vmem_limit_bytes=VMEM_MOST),
        name="pack_rows",
    )(queries, keys, values)


def gelu_parts(z, slope):
    square = z * z
    half = 0.5 * jnp.tanh(z * (GB * square + GA)) + 0.5
    act = z * half
    if not slope:
        return act, None
    return act, half + (act - act * half) * (6.0 * GB * square + 2.0 * GA)


def cutter(x):
    def cut(group, head, source, half):
        at = (2 * group + half) * WIDTH + head * HD
        return x[source, :, at : at + HD]

    return cut


def inner_kernel(
    me_ref, rate_ref, x_ref, first_ref, second_ref, inner,
    x, w1, w2, w1s, w2s, b1s, b2s, z1s, q1s, a_prev, g2_prev, b2_prev, xq_prev, sems, wsems,
):
    me = me_ref[0]
    copies = [pltpu.make_async_copy(x_ref, x, sems.at[0])]
    weights = [
        pltpu.make_async_copy(first_ref.at[pl.ds(me * LOCAL, LOCAL)], w1, wsems.at[0]),
        pltpu.make_async_copy(second_ref.at[pl.ds(me * LOCAL, LOCAL)], w2, wsems.at[1]),
    ]
    for copy in copies + weights:
        copy.start()
    for copy in copies + weights:
        copy.wait()
    cut = cutter(x)

    causal = lax.broadcasted_iota(jnp.int32, (CH, CH), 0) >= lax.broadcasted_iota(jnp.int32, (CH, CH), 1)

    def rms(value):
        return lax.rsqrt(lane_mean(value * value) + EPS)

    def stacked(head, q_source, q_half, k_source, k_half):
        q = cut(0, head, q_source, q_half)
        k = cut(1, head, k_source, k_half)
        rows = jnp.concatenate([q, k], axis=0)
        wide = rows.astype(f32)
        scale = rms(wide)
        return rows, wide * scale, scale

    def project(state, bias, rows, scale):
        high = state.astype(bf16)
        low = (state - high.astype(f32)).astype(bf16)
        both = dot(jnp.concatenate([rows, rows], axis=1), jnp.concatenate([high, low], axis=0))
        return both * scale + bias

    for head in range(LOCAL):
        w1s[head] = w1[head].astype(f32)
        start = w2[head].astype(f32)
        w2s[head] = start - jnp.mean(start, axis=0, keepdims=True)
        b1s[head] = jnp.zeros((1, FFI), f32)
        b2s[head] = jnp.zeros((1, HD), f32)
        b2_prev[head] = jnp.zeros((1, HD), f32)
        k = cut(1, head, 0, 0)
        z1s[head] = project(w1s[head], b1s[head], k, rms(k.astype(f32)))
        q1s[head] = jnp.zeros((CH, FFI), f32)
        a_prev[head] = jnp.zeros((CH + HD, FFI), bf16)
        g2_prev[head] = jnp.zeros((CH, HD), bf16)
        xq_prev[head] = jnp.zeros((CH, HD), f32)

    heads = range(LOCAL)
    etas = [rate_ref[me * LOCAL + head] * (1.0 / HD) for head in heads]

    def query_first():
        held = [(q1s[h], a_prev[h], g2_prev[h], b2_prev[h], xq_prev[h]) for h in heads]
        acts = [gelu_parts(held[h][0], False)[0] for h in heads]
        highs = [act.astype(bf16) for act in acts]
        lows = [(act - high.astype(f32)).astype(bf16) for act, high in zip(acts, highs)]
        boths = [dot_nt(highs[h], held[h][1]) for h in heads]
        rests = [dot_nt(lows[h], held[h][1][CH:]) for h in heads]
        return held, boths, rests

    def query_last(state):
        held, boths, rests = state
        seconds = [jnp.where(causal, both[:, :CH] + 1.0, 0.0).astype(bf16) for both in boths]
        outs = [boths[h][:, CH:] + rests[h] + held[h][3] - dot(seconds[h], held[h][2]) for h in heads]
        scales = [lax.rsqrt(lane_mean(out * out) + EPS) for out in outs]
        return [held[h][4] + outs[h] * scales[h] for h in heads]

    def one_block(source, half, next_source, next_half):
        z1 = [z1s[h] for h in heads]
        w2 = [w2s[h] for h in heads]
        b2 = [b2s[h] for h in heads]
        w1 = [w1s[h] for h in heads]
        b1 = [b1s[h] for h in heads]
        query = query_first()

        keys, targets, ahead, cross, normed_q = [], [], [], [], []
        for h in heads:
            k = cut(1, h, source, half).astype(f32)
            key = k * rms(k)
            target = cut(2, h, source, half).astype(f32) - key
            targets.append(target - lane_mean(target))
            keys.append(key.astype(bf16))
            rows, normed, scale = stacked(h, source, half, next_source, next_half)
            ahead.append(project(w1[h], b1[h], rows, scale))
            pair = dot_nt(normed.astype(bf16), keys[h]) + 1.0
            cross.append(jnp.concatenate([jnp.where(causal, pair[:CH], 0.0), pair[CH:]], axis=0).astype(bf16))
            normed_q.append(normed[:CH])

        parts = [gelu_parts(z, True) for z in z1]
        acts = [act.astype(bf16) for act, _ in parts]
        w2_low = [w.astype(bf16) for w in w2]
        cs = [dot_nt(acts[h], w2_low[h]) + b2[h] for h in heads]
        squares = [lane_mean(c * c) for c in cs]
        mixes = [lane_mean(c * target) for c, target in zip(cs, targets)]
        grads = []
        for h in heads:
            r = lax.rsqrt(squares[h] + EPS)
            grads.append((etas[h] * r) * (cs[h] * (r * (EPS * r * r + mixes[h] * r)) - targets[h]))
        grad_low = [grad.astype(bf16) for grad in grads]
        deeps = [dot(grad_low[h], w2_low[h]) * parts[h][1] for h in heads]
        deep_low = [deep.astype(bf16) for deep in deeps]
        boths = [ahead[h] - dot(cross[h], deep_low[h]) for h in heads]
        new_w2 = [w2[h] - dot_tn(grad_low[h], acts[h]) for h in heads]
        new_b2 = [b2[h] - jnp.sum(grads[h], axis=0, keepdims=True) for h in heads]
        new_w1 = [w1[h] - dot_tn(keys[h], deep_low[h]) for h in heads]
        new_b1 = [b1[h] - jnp.sum(deeps[h], axis=0, keepdims=True) for h in heads]
        done = query_last(query)

        for h in heads:
            z1s[h] = boths[h][CH:]
            q1s[h] = boths[h][:CH]
            a_prev[h, :CH, :] = acts[h]
            a_prev[h, CH:, :] = w2_low[h]
            g2_prev[h] = grad_low[h]
            b2_prev[h] = b2[h]
            xq_prev[h] = normed_q[h]
            w1s[h] = new_w1[h]
            b1s[h] = new_b1[h]
            w2s[h] = new_w2[h]
            b2s[h] = new_b2[h]
        return done

    def blocks(source, carry):
        done = one_block(source, 0, source, 1)
        for h in heads:
            inner[jnp.maximum(source - 1, 0), :, WIDTH + h * HD : WIDTH + (h + 1) * HD] = done[h]
        done = one_block(source, 1, jnp.minimum(source + 1, PARTS - 1), 0)
        for h in heads:
            inner[source, :, h * HD : (h + 1) * HD] = done[h]
        return carry

    lax.fori_loop(0, PARTS, blocks, 0)
    done = query_last(query_first())
    for h in heads:
        inner[PARTS - 1, :, WIDTH + h * HD : WIDTH + (h + 1) * HD] = done[h]


VMEM = pl.BlockSpec(memory_space=pltpu.VMEM)
SMEM = pl.BlockSpec(memory_space=pltpu.SMEM)
HBM = pl.BlockSpec(memory_space=pl.ANY)


def run_inner(me, rate, pieces, first, second):
    return pl.pallas_call(
        inner_kernel,
        out_shape=jax.ShapeDtypeStruct((PARTS, CH, 2 * WIDTH), f32),
        in_specs=[SMEM, SMEM, HBM, HBM, HBM],
        out_specs=VMEM,
        scratch_shapes=[
            pltpu.VMEM((PARTS, CH, 6 * WIDTH), bf16),
            pltpu.VMEM((LOCAL, HD, FFI), bf16),
            pltpu.VMEM((LOCAL, HD, FFI), bf16),
            pltpu.VMEM((LOCAL, HD, FFI), f32),
            pltpu.VMEM((LOCAL, HD, FFI), f32),
            pltpu.VMEM((LOCAL, 1, FFI), f32),
            pltpu.VMEM((LOCAL, 1, HD), f32),
            pltpu.VMEM((LOCAL, CH, FFI), f32),
            pltpu.VMEM((LOCAL, CH, FFI), f32),
            pltpu.VMEM((LOCAL, CH + HD, FFI), bf16),
            pltpu.VMEM((LOCAL, CH, HD), bf16),
            pltpu.VMEM((LOCAL, 1, HD), f32),
            pltpu.VMEM((LOCAL, CH, HD), f32),
            pltpu.SemaphoreType.DMA((1,)),
            pltpu.SemaphoreType.DMA((2,)),
        ],
        compiler_params=pltpu.CompilerParams(vmem_limit_bytes=VMEM_MOST),
        cost_estimate=pl.CostEstimate(flops=4_000_000_000, bytes_accessed=100_000_000, transcendentals=0),
        name="run_inner",
    )(me, rate, pieces, first, second)


def attend_kernel(steps, me_ref, *rest):
    count = len(steps)
    x_ref, seg_ref, gate_ref, inner_ref = rest[:4]
    outs = rest[4 : 4 + count]
    x, inner, k_aug, v_aug, mixed, sems, isems = rest[4 + count :]
    me = me_ref[0]
    targets = [target_of(me, step) for step in steps]
    copies = [pltpu.make_async_copy(x_ref, x, sems.at[0])] + [
        pltpu.make_async_copy(inner_ref.at[target], inner.at[i], isems.at[i]) for i, target in enumerate(targets)
    ]
    for copy in copies:
        copy.start()
    for copy in copies:
        copy.wait()
    cut = cutter(x)
    ones = jnp.ones((CH, HD), bf16)

    def prepare(source, carry):
        for half in range(2):
            rows = pl.ds(pl.multiple_of(source * TOK + half * CH, CH), CH)
            for head in range(LOCAL):
                k_aug[head, rows, :] = jnp.concatenate([cut(1, head, source, half), seg_ref[rows, :]], axis=1)
                v_aug[head, rows, :] = jnp.concatenate([cut(2, head, source, half), ones], axis=1)
        return carry

    lax.fori_loop(0, PARTS, prepare, 0)
    gates = [jnp.tanh(gate_ref[me * LOCAL + head]) for head in range(LOCAL)]
    for i, target in enumerate(targets):
        seg = seg_ref[pl.ds(pl.multiple_of(target * TOK, TOK), TOK), :]
        for head in range(LOCAL):
            q = jnp.concatenate([cut(0, head, target, half) for half in range(2)], axis=0)
            q = jnp.concatenate([(q * 0.125).astype(bf16), seg], axis=1)
            scores = dot_nt(q, k_aug[head])
            top = jnp.max(scores, axis=-1, keepdims=True)
            got = dot(jnp.exp(scores - top).astype(bf16), v_aug[head])
            got = got[:, :HD] / got[:, HD:]
            for half in range(2):
                at = slice(half * WIDTH + head * HD, half * WIDTH + (head + 1) * HD)
                part = got[half * CH : (half + 1) * CH] + gates[head] * inner[i, :, at]
                mixed[i, :, at] = part.astype(bf16)
    copies = [pltpu.make_async_copy(mixed.at[i], outs[i], isems.at[i]) for i in range(count)]
    for copy in copies:
        copy.start()
    for copy in copies:
        copy.wait()


def run_attend(steps, me, pieces, seg, gate, inner):
    count = len(steps)
    return pl.pallas_call(
        functools.partial(attend_kernel, steps),
        out_shape=[jax.ShapeDtypeStruct((CH, 2 * WIDTH), bf16)] * count,
        in_specs=[SMEM, HBM, VMEM, VMEM, HBM],
        out_specs=[HBM] * count,
        scratch_shapes=[
            pltpu.VMEM((PARTS, CH, 6 * WIDTH), bf16),
            pltpu.VMEM((count, CH, 2 * WIDTH), f32),
            pltpu.VMEM((LOCAL, LEN, 2 * HD), bf16),
            pltpu.VMEM((LOCAL, LEN, 2 * HD), bf16),
            pltpu.VMEM((count, CH, 2 * WIDTH), bf16),
            pltpu.SemaphoreType.DMA((1,)),
            pltpu.SemaphoreType.DMA((count,)),
        ],
        compiler_params=pltpu.CompilerParams(vmem_limit_bytes=VMEM_MOST),
        cost_estimate=pl.CostEstimate(flops=100_000_000 * count, bytes_accessed=2_500_000 * count, transcendentals=0),
        name="run_attend",
    )(me, pieces, seg, gate, inner)


def project_kernel(place_ref, *rest):
    mixed = rest[:PARTS]
    own, sib = rest[PARTS : PARTS + 4], rest[PARTS + 4 : PARTS + 8]
    out, held, weight, sems, wsems = rest[PARTS + 8 :]
    me, dp = place_ref[0], place_ref[1]
    core = lax.rem(me, 2)
    y, x = dp // 8, lax.rem(dp // 2, 4)
    wide = weight.shape[2]
    loads = []
    for side, blocks in enumerate((own, sib)):
        axis = core if side == 0 else 1 - core
        for i, far in enumerate(STEPS):
            for j, near in enumerate(STEPS):
                dx = jnp.where(axis == 0, near, far)
                dy = jnp.where(axis == 0, far, near)
                line = lax.rem(y + 4 - dy, 4) * 4 + lax.rem(x + 4 - dx, 4)
                loads.append(
                    pltpu.make_async_copy(
                        blocks[i].at[pl.ds(j * 2 * ROWS, 2 * ROWS)],
                        weight.at[side, pl.ds(pl.multiple_of(line * 2 * ROWS, 2 * ROWS), 2 * ROWS)],
                        wsems.at[side, 4 * i + j],
                    )
                )
    copies = [
        pltpu.make_async_copy(mixed[step], held.at[source_of(me, step)], sems.at[step]) for step in range(PARTS)
    ]
    for copy in copies + loads:
        copy.start()
    for copy in copies:
        copy.wait()
    rows = [
        jnp.concatenate([held[part, :, half * WIDTH : (half + 1) * WIDTH] for part in range(PARTS)], axis=1)
        for half in range(2)
    ]
    rows = jnp.concatenate(rows, axis=0)
    for side in range(2):
        for copy in loads[16 * side : 16 * side + 16]:
            copy.wait()
        axis = core if side == 0 else 1 - core
        for at in range(0, wide, 256):
            to = pl.multiple_of(axis * wide + at, 256)
            out[:, pl.ds(to, 256)] = dot(rows, weight[side, :, at : at + 256]).astype(bf16)


def run_project(place, mixed, own, sib):
    hbm = pl.BlockSpec(memory_space=pl.ANY)
    wide = own[0].shape[1]
    return pl.pallas_call(
        project_kernel,
        out_shape=jax.ShapeDtypeStruct((TOK, 2 * wide), bf16),
        in_specs=[pl.BlockSpec(memory_space=pltpu.SMEM)] + [hbm] * (PARTS + 8),
        out_specs=pl.BlockSpec(memory_space=pltpu.VMEM),
        scratch_shapes=[
            pltpu.VMEM((PARTS, CH, 2 * WIDTH), bf16),
            pltpu.VMEM((2, HH, wide), bf16),
            pltpu.SemaphoreType.DMA((PARTS,)),
            pltpu.SemaphoreType.DMA((2, 16)),
        ],
        compiler_params=pltpu.CompilerParams(vmem_limit_bytes=VMEM_MOST),
        name="project_rows",
    )(place, *mixed, *own, *sib)


ROWS = HH // 32
STEPS = (0, 1, 3, 2)


def where_is(index):
    dp, seq = divmod(index, PARTS)
    return dp // 8, (dp // 2) % 4, dp % 2, seq // 2, seq % 2


def index_of(y, x, z, group, core):
    return ((y % 4) * 8 + (x % 4) * 2 + z % 2) * PARTS + (group % 4) * 2 + core % 2


def move(array, place):
    pairs = [(i, index_of(*place(*where_is(i)))) for i in range(32 * PARTS)]
    return lax.ppermute(array, ("dp", "seq"), pairs)


def turn(array, step):
    return lax.ppermute(array, "seq", [(i, (i + step) % PARTS) for i in range(PARTS)])


def near_axis(step):
    return lambda y, x, z, group, core: (y + step * core, x + step * (1 - core), z, group, core)


def far_axis(step):
    return lambda y, x, z, group, core: (y + step * (1 - core), x + step * core, z, group, core)


def flip_z(y, x, z, group, core):
    return y, x, 1 - z, group, core


def flip_core(y, x, z, group, core):
    return y, x, z, group, 1 - core


GROUPS = ((1, 2, 3, 4, 5, 6, 7), (0,))


def after(value, *first):
    return lax.optimization_barrier((value, *first))[0]


def other_chip(step, swap):
    return lambda y, x, z, group, core: (y, x, z, group + step, (core + swap) % 2)


def on_device(
    queries, key_states, value_states, segment_ids, inner_first, inner_second, inner_rate, branch_gate, out_weight
):
    seq, dp = lax.axis_index("seq"), lax.axis_index("dp")
    place = jnp.stack([seq, dp]).astype(jnp.int32)
    wide = out_weight.shape[1] // 2
    slab = lax.dynamic_slice_in_dim(out_weight, (seq % 2) * wide, wide, 1)
    other = move(slab, flip_z)
    upper = dp % 2 == 1
    slab = jnp.concatenate([jnp.where(upper, other, slab), jnp.where(upper, slab, other)], axis=0)

    pieces = pack(queries[0], key_states[0], value_states[0])
    pieces = lax.all_to_all(pieces, "seq", split_axis=0, concat_axis=0, tiled=True)
    near = [move(slab, near_axis(step)) for step in STEPS[1:]]
    slab = jnp.concatenate([slab] + near, axis=0)
    own = [slab] + [move(slab, far_axis(step)) for step in STEPS[1:]]
    sib = [move(slab, flip_core)]

    seg = jnp.where(segment_ids[0][:, None] == jnp.arange(HD)[None, :], SAME, 0.0).astype(bf16)
    gate = branch_gate.reshape(-1, 1, HD)
    pieces, slab, seg, gate = lax.optimization_barrier((pieces, slab, seg, gate))
    inner = run_inner(place, inner_rate, pieces, inner_first, inner_second)
    inner, *own = lax.optimization_barrier((inner, *own))
    sib += [move(block, flip_core) for block in own[1:]]
    mixed = [None] * PARTS
    for turn, steps in enumerate(GROUPS):
        group = run_attend(steps, place, pieces, seg, gate, inner)
        if turn == 0:
            group, sib, inner = lax.optimization_barrier((group, sib, inner))
        for step, piece in zip(steps, group):
            mixed[step] = move(piece, other_chip(*MOVES[step - 1])) if step else piece
    return run_project(place, mixed, own, sib)[None]


def solution(mesh):
    in_specs = (
        P("dp", "seq", None),
        P("dp", "seq", None),
        P("dp", "seq", None),
        P("dp", None),
        P(),
        P(),
        P(),
        P(),
        P("dp", None),
    )
    return jax.shard_map(
        on_device, mesh=mesh, in_specs=in_specs, out_specs=P("dp", "seq", None), check_vma=False
    )
```

```python
import functools
import math

import jax
import jax.numpy as jnp
from jax import lax
from jax.experimental import pallas as pl
from jax.experimental.pallas import tpu as pltpu
from jax.sharding import PartitionSpec as P

HD = 64
FFI = 256
CH = 64
BATCH = 4
LOCAL = 3
PARTS = 8
TOK = 128
LEN = 1024
HH = 1536
WIDTH = LOCAL * HD
SAME = 32.0
EPS = 1e-6
GA = math.sqrt(2.0 / math.pi)
GB = GA * 0.044715
MIB = 1024 * 1024

f32 = jnp.float32
bf16 = jnp.bfloat16


def dot(left, right):
    return jnp.dot(left, right, preferred_element_type=f32)


def dot_nt(left, right):
    return lax.dot_general(left, right, (((1,), (1,)), ((), ())), preferred_element_type=f32)


def dot_tn(left, right):
    return lax.dot_general(left, right, (((0,), (0,)), ((), ())), preferred_element_type=f32)


def lane_mean(value):
    return jnp.mean(value, axis=-1, keepdims=True)


def pack_kernel(q_ref, k_ref, v_ref, weight_ref, out, slab):
    wide = slab.shape[1]
    core = lax.rem(lax.axis_index("seq"), 2)
    slab[...] = weight_ref[:, pl.ds(pl.multiple_of(core * wide, wide), wide)]
    for part in range(PARTS):
        cols = slice(part * WIDTH, (part + 1) * WIDTH)
        for group, ref in enumerate((q_ref, k_ref, v_ref)):
            for half in range(2):
                at = (2 * group + half) * WIDTH
                out[part, :, at : at + WIDTH] = ref[half * CH : (half + 1) * CH, cols]


def pack(queries, keys, values, weight):
    return pl.pallas_call(
        pack_kernel,
        out_shape=[
            jax.ShapeDtypeStruct((PARTS, CH, 6 * WIDTH), bf16),
            jax.ShapeDtypeStruct((weight.shape[0], weight.shape[1] // 2), bf16),
        ],
        compiler_params=pltpu.CompilerParams(vmem_limit_bytes=62 * MIB),
        name="pack_rows",
    )(queries, keys, values, weight)


def gelu_parts(z, slope):
    square = z * z
    half = 0.5 * jnp.tanh(z * (GB * square + GA)) + 0.5
    act = z * half
    if not slope:
        return act, None
    return act, half + (act - act * half) * (6.0 * GB * square + 2.0 * GA)


def stack_heads(joint):
    head = lax.broadcasted_iota(jnp.int32, joint.shape, 1) // HD
    zero = jnp.zeros_like(joint)
    return jnp.concatenate([jnp.where(head == h, joint, zero) for h in range(LOCAL)], axis=0)


def join_heads(full):
    rows = full.shape[0] // LOCAL
    blocks = [full[h * rows : (h + 1) * rows] for h in range(LOCAL)]
    head = lax.broadcasted_iota(jnp.int32, blocks[0].shape, 1) // HD
    joint = blocks[0]
    for h in range(1, LOCAL):
        joint = jnp.where(head == h, blocks[h], joint)
    return joint


def halves(value):
    high = value.astype(bf16)
    return high, (value - high.astype(f32)).astype(bf16)


def head_means(value, spread):
    rows = value.shape[0]
    both = dot(jnp.concatenate(halves(value), axis=0), spread)
    return both[:rows] + both[rows:]


def heads_kernel(
    rate_ref, x, seg_ref, weights, gate_ref, mixed,
    q_low, k_low, q_wide, k_wide, xq, target, attended, w1s, w2s, b1s, b2s, z1s, q1s, a_prev,
    w2_prev, g2_prev, b2_prev,
):
    me = lax.axis_index("seq")
    heads = range(LOCAL)
    column = lax.broadcasted_iota(jnp.int32, (WIDTH, WIDTH), 1) // HD
    row = lax.broadcasted_iota(jnp.int32, (WIDTH, WIDTH), 0) // HD
    spread = jnp.where(row == column, 1.0 / HD, 0.0).astype(bf16)
    token = lax.broadcasted_iota(jnp.int32, (CH, WIDTH), 0)
    causal = token >= lax.rem(lax.broadcasted_iota(jnp.int32, (CH, WIDTH), 1), HD)
    lane_head = lax.broadcasted_iota(jnp.int32, (1, WIDTH), 1) // HD
    etas = jnp.zeros((1, WIDTH), f32)
    for h in heads:
        etas = jnp.where(lane_head == h, rate_ref[me * LOCAL + h] * (1.0 / HD), etas)

    half_rows = PARTS * CH
    number = lax.broadcasted_iota(jnp.int32, (HD, LEN), 0)
    unit = jnp.where(
        lax.broadcasted_iota(jnp.int32, (HD, HD), 0) == lax.broadcasted_iota(jnp.int32, (HD, HD), 1), 1.0, 0.0
    )
    seg = dot_tn(jnp.where(seg_ref[...] == number, SAME, 0.0).astype(bf16), unit.astype(bf16)).astype(bf16)
    seg = seg.reshape(PARTS, 2, CH, HD)
    segs = [seg[:, half].reshape(half_rows, HD) for half in range(2)]

    def columns(group, h, half):
        at = (2 * group + half) * WIDTH + h * HD
        return x[:, :, at : at + HD].reshape(half_rows, HD)

    ones = jnp.ones((half_rows, HD), bf16)
    for h in heads:
        keys = [jnp.concatenate([columns(1, h, half), segs[half]], axis=1) for half in range(2)]
        values = [jnp.concatenate([columns(2, h, half), ones], axis=1) for half in range(2)]
        keys, values = jnp.concatenate(keys, axis=0), jnp.concatenate(values, axis=0)
        for half in range(2):
            q = jnp.concatenate([(columns(0, h, half) * 0.125).astype(bf16), segs[half]], axis=1)
            scores = dot_nt(q, keys)
            top = jnp.max(scores, axis=-1, keepdims=True)
            got = dot(jnp.exp(scores - top).astype(bf16), values)
            got = got[:, :HD] / got[:, HD:]
            attended[:, half, :, h * HD : (h + 1) * HD] = got.reshape(PARTS, CH, HD)

    for begin in range(0, PARTS, BATCH):
        some = slice(begin, begin + BATCH)
        for half in range(2):
            q, k, v = (
                x[some, :, (2 * g + half) * WIDTH : (2 * g + half + 1) * WIDTH].reshape(BATCH * CH, WIDTH)
                for g in range(3)
            )
            both = jnp.concatenate([q, k], axis=0).astype(f32)
            both = both * lax.rsqrt(head_means(both * both, spread) + EPS)
            high, low = halves(both)
            goal = v.astype(f32) - both[BATCH * CH :]
            goal = goal - head_means(goal, spread)
            per_block = (BATCH, CH, WIDTH)
            xq[some, half] = both[: BATCH * CH].reshape(per_block)
            target[some, half] = goal.reshape(per_block)
            q_low[some, half] = high[: BATCH * CH].reshape(per_block)
            k_low[some, half] = high[BATCH * CH :].reshape(per_block)
            for h in heads:
                at = slice(h * HD, (h + 1) * HD)
                wide = jnp.concatenate([high[:, at], low[:, at], high[:, at]], axis=1)
                q_wide[h, some, half] = wide[: BATCH * CH].reshape(per_block)
                k_wide[h, some, half] = wide[BATCH * CH :].reshape(per_block)

    def project(h, state, bias, wide):
        high, low = halves(state)
        return dot(wide, jnp.concatenate([high, high, low], axis=0)) + bias

    for h in heads:
        at = slice(h * HD, (h + 1) * HD)
        start = weights[1, h].astype(f32)
        w2s[at, :] = start - jnp.mean(start, axis=0, keepdims=True)
        first = weights[0, h]
        w1s[at, :] = first.astype(f32)
        z1s[at, :] = dot(k_wide[h, 0, 0], jnp.concatenate([first, first, jnp.zeros_like(first)], axis=0))
    for ref in (b1s, b2s, q1s, a_prev, w2_prev, g2_prev, b2_prev):
        ref[...] = jnp.zeros_like(ref)

    gate = jnp.tanh(gate_ref[...])

    def query_first():
        high, low = halves(gelu_parts(q1s[...], False)[0])
        near = dot_nt(high, a_prev[...])
        deep = dot_nt(jnp.concatenate([high, low], axis=0), w2_prev[...])
        return near, deep, g2_prev[...], b2_prev[...]

    def query_last(state, source, half):
        near, deep, grad, bias = state
        near = jnp.where(causal, join_heads(near) + 1.0, 0.0).astype(bf16)
        out = join_heads(deep[:WIDTH] + deep[WIDTH:]) + bias - dot(near, grad)
        inner = xq[source, half] + out * lax.rsqrt(head_means(out * out, spread) + EPS)
        mixed[source, :, half * WIDTH : (half + 1) * WIDTH] = (attended[source, half] + gate * inner).astype(bf16)

    def one_block(now, later, before):
        z1, w1_now, w2_now, b1, b2 = z1s[...], w1s[...], w2s[...], b1s[...], b2s[...]
        goal = target[*now]
        query = query_first()

        keys = stack_heads(k_low[*now])
        cross = dot_nt(jnp.concatenate([q_low[*now], k_low[*later]], axis=0), keys) + 1.0
        cross = jnp.concatenate([jnp.where(causal, cross[:CH], 0.0), cross[CH:]], axis=0).astype(bf16)
        cross = stack_heads(cross)
        ahead = [
            project(
                h,
                w1_now[h * HD : (h + 1) * HD],
                b1[h],
                jnp.concatenate([q_wide[h, *now], k_wide[h, *later]], axis=0),
            )
            for h in heads
        ]

        act, slope = gelu_parts(z1, True)
        act_low = act.astype(bf16)
        w2_low = w2_now.astype(bf16)
        c = join_heads(dot_nt(act_low, w2_low)) + b2
        means = dot(jnp.concatenate([c * c, c * goal], axis=0).astype(bf16), spread)
        r = lax.rsqrt(means[:CH] + EPS)
        grad = (etas * r) * (c * (r * (EPS * r * r + means[CH:] * r)) - goal)
        grad_low = stack_heads(grad.astype(bf16))
        deep = dot(grad_low, w2_low) * slope
        deep_low = deep.astype(bf16)
        moved = dot(cross, deep_low)
        new_w2 = w2_now - dot_tn(grad_low, act_low)
        new_w1 = w1_now - dot_tn(keys, deep_low)
        new_b2 = b2 - jnp.sum(grad, axis=0, keepdims=True)
        new_b1 = [b1[h] - jnp.sum(deep[h * CH : (h + 1) * CH], axis=0, keepdims=True) for h in heads]
        query_last(query, *before)

        for h in heads:
            both = ahead[h] - moved[2 * h * CH : 2 * (h + 1) * CH]
            q1s[h * CH : (h + 1) * CH, :] = both[:CH]
            z1s[h * CH : (h + 1) * CH, :] = both[CH:]
            b1s[h] = new_b1[h]
        a_prev[...] = act_low
        w2_prev[...] = w2_low
        g2_prev[...] = grad_low
        b2_prev[...] = b2
        w1s[...] = new_w1
        w2s[...] = new_w2
        b2s[...] = new_b2

    def blocks(source, carry):
        last, ahead = jnp.maximum(source - 1, 0), jnp.minimum(source + 1, PARTS - 1)
        one_block((source, 0), (source, 1), (last, 1))
        one_block((source, 1), (ahead, 0), (source, 0))
        return carry

    lax.fori_loop(0, PARTS, blocks, 0)
    query_last(query_first(), PARTS - 1, 1)


VMEM = pl.BlockSpec(memory_space=pltpu.VMEM)
SMEM = pl.BlockSpec(memory_space=pltpu.SMEM)


def run_heads(rate, pieces, seg, weights, gate):
    blocks = (PARTS, 2, CH, WIDTH)
    return pl.pallas_call(
        heads_kernel,
        out_shape=jax.ShapeDtypeStruct((PARTS, CH, 2 * WIDTH), bf16),
        in_specs=[SMEM] + [VMEM] * 4,
        out_specs=VMEM,
        scratch_shapes=[
            pltpu.VMEM(blocks, bf16),
            pltpu.VMEM(blocks, bf16),
            pltpu.VMEM((LOCAL,) + blocks, bf16),
            pltpu.VMEM((LOCAL,) + blocks, bf16),
            pltpu.VMEM(blocks, f32),
            pltpu.VMEM(blocks, f32),
            pltpu.VMEM(blocks, f32),
            pltpu.VMEM((WIDTH, FFI), f32),
            pltpu.VMEM((WIDTH, FFI), f32),
            pltpu.VMEM((LOCAL, 1, FFI), f32),
            pltpu.VMEM((1, WIDTH), f32),
            pltpu.VMEM((WIDTH, FFI), f32),
            pltpu.VMEM((WIDTH, FFI), f32),
            pltpu.VMEM((WIDTH, FFI), bf16),
            pltpu.VMEM((WIDTH, FFI), bf16),
            pltpu.VMEM((WIDTH, WIDTH), bf16),
            pltpu.VMEM((1, WIDTH), f32),
        ],
        compiler_params=pltpu.CompilerParams(vmem_limit_bytes=32 * MIB),
        cost_estimate=pl.CostEstimate(flops=4_000_000_000, bytes_accessed=100_000_000, transcendentals=0),
        name="run_heads",
    )(rate, pieces, seg, weights, gate)


def project_kernel(mixed, *rest):
    own, sib, out, groups = rest[:4], rest[4:8], rest[8], rest[9]
    core, dp = lax.rem(lax.axis_index("seq"), 2), lax.axis_index("dp")
    y, x = dp // 8, lax.rem(dp // 2, 4)
    for source in range(PARTS):
        for pair in range(2):
            for half in range(2):
                at = half * WIDTH + pair * 2 * ROWS
                groups[2 * source + pair, half * CH : (half + 1) * CH, :] = mixed[source, :, at : at + 2 * ROWS]
    for side, blocks in enumerate((own, sib)):
        axis = core if side == 0 else 1 - core
        left = []
        for far in STEPS:
            for near in STEPS:
                dx = jnp.where(axis == 0, near, far)
                dy = jnp.where(axis == 0, far, near)
                left.append(groups[lax.rem(y + 4 - dy, 4) * 4 + lax.rem(x + 4 - dx, 4)])
        left = jnp.concatenate(left, axis=1)
        wide = blocks[0].shape[1]
        for at in range(0, wide, 256):
            right = jnp.concatenate([block[:, at : at + 256] for block in blocks], axis=0)
            out[:, pl.ds(pl.multiple_of(axis * wide + at, 256), 256)] = dot(left, right).astype(bf16)


def run_project(mixed, own, sib):
    wide = own[0].shape[1]
    return pl.pallas_call(
        project_kernel,
        out_shape=jax.ShapeDtypeStruct((TOK, 2 * wide), bf16),
        in_specs=[VMEM] * 9,
        out_specs=VMEM,
        scratch_shapes=[pltpu.VMEM((2 * PARTS, TOK, 2 * ROWS), bf16)],
        compiler_params=pltpu.CompilerParams(vmem_limit_bytes=20 * MIB),
        name="project_rows",
    )(mixed, *own, *sib)


ROWS = HH // 32
STEPS = (0, 1, 3, 2)


def where_is(index):
    dp, seq = divmod(index, PARTS)
    return dp // 8, (dp // 2) % 4, dp % 2, seq // 2, seq % 2


def index_of(y, x, z, group, core):
    return ((y % 4) * 8 + (x % 4) * 2 + z % 2) * PARTS + (group % 4) * 2 + core % 2


def move(array, place):
    pairs = [(i, index_of(*place(*where_is(i)))) for i in range(32 * PARTS)]
    return lax.ppermute(array, ("dp", "seq"), pairs)


def turn(array, step):
    return lax.ppermute(array, "seq", [(i, (i + step) % PARTS) for i in range(PARTS)])


def near_axis(step):
    return lambda y, x, z, group, core: (y + step * core, x + step * (1 - core), z, group, core)


def far_axis(step):
    return lambda y, x, z, group, core: (y + step * (1 - core), x + step * core, z, group, core)


def flip_z(y, x, z, group, core):
    return y, x, 1 - z, group, core


def flip_core(y, x, z, group, core):
    return y, x, z, group, 1 - core


def on_device(
    queries, key_states, value_states, segment_ids, inner_first, inner_second, inner_rate, branch_gate, out_weight
):
    seq, dp = lax.axis_index("seq"), lax.axis_index("dp")
    pieces, slab = pack(queries[0], key_states[0], value_states[0], out_weight)
    other = move(slab, flip_z)
    upper = dp % 2 == 1
    slab = jnp.concatenate([jnp.where(upper, other, slab), jnp.where(upper, slab, other)], axis=0)

    pieces = lax.all_to_all(pieces, "seq", split_axis=0, concat_axis=0, tiled=True)
    near = [move(slab, near_axis(step)) for step in STEPS[1:]]
    slab = jnp.concatenate([slab] + near, axis=0)
    own = [slab] + [move(slab, far_axis(step)) for step in STEPS[1:]]
    sib = [move(slab, flip_core)]

    weights = jnp.stack([lax.dynamic_slice_in_dim(w, seq * LOCAL, LOCAL, 0) for w in (inner_first, inner_second)])
    gate = lax.dynamic_slice_in_dim(branch_gate, seq * WIDTH, WIDTH, 0)[None]
    pieces, slab, gate, weights = lax.optimization_barrier((pieces, slab, gate, weights))
    mixed = run_heads(inner_rate, pieces, segment_ids, weights, gate)
    own = list(lax.optimization_barrier((tuple(own), mixed))[0])
    mixed = lax.all_to_all(mixed, "seq", split_axis=0, concat_axis=0, tiled=True)
    sib = [move(block, flip_core) for block in own]
    return run_project(mixed, own, sib)[None]


def solution(mesh):
    in_specs = (
        P("dp", "seq", None),
        P("dp", "seq", None),
        P("dp", "seq", None),
        P("dp", None),
        P(),
        P(),
        P(),
        P(),
        P("dp", None),
    )
    return jax.shard_map(
        on_device, mesh=mesh, in_specs=in_specs, out_specs=P("dp", "seq", None), check_vma=False
    )
```

```python
import functools
import math

import jax
import jax.numpy as jnp
from jax import lax
from jax.experimental import pallas as pl
from jax.experimental.pallas import tpu as pltpu
from jax.sharding import PartitionSpec as P

HD = 64
FFI = 256
CH = 64
BATCH = 4
LOCAL = 3
PARTS = 8
TOK = 128
LEN = 1024
HH = 1536
WIDTH = LOCAL * HD
SAME = 32.0
EPS = 1e-6
GA = math.sqrt(2.0 / math.pi)
GB = GA * 0.044715
MIB = 1024 * 1024

f32 = jnp.float32
bf16 = jnp.bfloat16


def dot(left, right):
    return jnp.dot(left, right, preferred_element_type=f32)


def dot_nt(left, right):
    return lax.dot_general(left, right, (((1,), (1,)), ((), ())), preferred_element_type=f32)


def dot_tn(left, right):
    return lax.dot_general(left, right, (((0,), (0,)), ((), ())), preferred_element_type=f32)


def lane_mean(value):
    return jnp.mean(value, axis=-1, keepdims=True)


def pack_kernel(q_ref, k_ref, v_ref, weight_ref, out, slab):
    wide = slab.shape[1]
    core = lax.rem(lax.axis_index("seq"), 2)
    slab[...] = weight_ref[:, pl.ds(pl.multiple_of(core * wide, wide), wide)]
    for part in range(PARTS):
        cols = slice(part * WIDTH, (part + 1) * WIDTH)
        for group, ref in enumerate((q_ref, k_ref, v_ref)):
            for half in range(2):
                at = (2 * group + half) * WIDTH
                out[part, :, at : at + WIDTH] = ref[half * CH : (half + 1) * CH, cols]


def pack(queries, keys, values, weight):
    return pl.pallas_call(
        pack_kernel,
        out_shape=[
            jax.ShapeDtypeStruct((PARTS, CH, 6 * WIDTH), bf16),
            jax.ShapeDtypeStruct((weight.shape[0], weight.shape[1] // 2), bf16),
        ],
        compiler_params=pltpu.CompilerParams(vmem_limit_bytes=62 * MIB),
        name="pack_rows",
    )(queries, keys, values, weight)


def gelu_parts(z, slope):
    square = z * z
    half = 0.5 * jnp.tanh(z * (GB * square + GA)) + 0.5
    act = z * half
    if not slope:
        return act, None
    return act, half + (act - act * half) * (6.0 * GB * square + 2.0 * GA)


def stack_heads(joint):
    head = lax.broadcasted_iota(jnp.int32, joint.shape, 1) // HD
    zero = jnp.zeros_like(joint)
    return jnp.concatenate([jnp.where(head == h, joint, zero) for h in range(LOCAL)], axis=0)


def join_heads(full):
    rows = full.shape[0] // LOCAL
    blocks = [full[h * rows : (h + 1) * rows] for h in range(LOCAL)]
    head = lax.broadcasted_iota(jnp.int32, blocks[0].shape, 1) // HD
    joint = blocks[0]
    for h in range(1, LOCAL):
        joint = jnp.where(head == h, blocks[h], joint)
    return joint


def halves(value):
    high = value.astype(bf16)
    return high, (value - high.astype(f32)).astype(bf16)


def head_means(value, spread):
    rows = value.shape[0]
    both = dot(jnp.concatenate(halves(value), axis=0), spread)
    return both[:rows] + both[rows:]


def heads_kernel(
    rate_ref, x, seg_ref, weights, gate_ref, mixed,
    q_low, k_low, q_wide, k_wide, xq, target, attended, w1s, w2s, b1s, b2s, z1s, q1s, a_prev,
    w2_prev, g2_prev, b2_prev,
):
    me = lax.axis_index("seq")
    heads = range(LOCAL)
    column = lax.broadcasted_iota(jnp.int32, (WIDTH, WIDTH), 1) // HD
    row = lax.broadcasted_iota(jnp.int32, (WIDTH, WIDTH), 0) // HD
    spread = jnp.where(row == column, 1.0 / HD, 0.0).astype(bf16)
    token = lax.broadcasted_iota(jnp.int32, (CH, WIDTH), 0)
    causal = token >= lax.rem(lax.broadcasted_iota(jnp.int32, (CH, WIDTH), 1), HD)
    lane_head = lax.broadcasted_iota(jnp.int32, (1, WIDTH), 1) // HD
    etas = jnp.zeros((1, WIDTH), f32)
    for h in heads:
        etas = jnp.where(lane_head == h, rate_ref[me * LOCAL + h] * (1.0 / HD), etas)

    half_rows = PARTS * CH
    number = lax.broadcasted_iota(jnp.int32, (HD, LEN), 0)
    unit = jnp.where(
        lax.broadcasted_iota(jnp.int32, (HD, HD), 0) == lax.broadcasted_iota(jnp.int32, (HD, HD), 1), 1.0, 0.0
    )
    seg = dot_tn(jnp.where(seg_ref[...] == number, SAME, 0.0).astype(bf16), unit.astype(bf16)).astype(bf16)
    seg = seg.reshape(PARTS, 2, CH, HD)
    segs = [seg[:, half].reshape(half_rows, HD) for half in range(2)]

    def columns(group, h, half):
        at = (2 * group + half) * WIDTH + h * HD
        return x[:, :, at : at + HD].reshape(half_rows, HD)

    ones = jnp.ones((half_rows, HD), bf16)
    for h in heads:
        keys = [jnp.concatenate([columns(1, h, half), segs[half]], axis=1) for half in range(2)]
        values = [jnp.concatenate([columns(2, h, half), ones], axis=1) for half in range(2)]
        keys, values = jnp.concatenate(keys, axis=0), jnp.concatenate(values, axis=0)
        for half in range(2):
            q = jnp.concatenate([(columns(0, h, half) * 0.125).astype(bf16), segs[half]], axis=1)
            scores = dot_nt(q, keys)
            top = jnp.max(scores, axis=-1, keepdims=True)
            got = dot(jnp.exp(scores - top).astype(bf16), values)
            got = got[:, :HD] / got[:, HD:]
            attended[:, half, :, h * HD : (h + 1) * HD] = got.reshape(PARTS, CH, HD)

    for begin in range(0, PARTS, BATCH):
        some = slice(begin, begin + BATCH)
        for half in range(2):
            q, k, v = (
                x[some, :, (2 * g + half) * WIDTH : (2 * g + half + 1) * WIDTH].reshape(BATCH * CH, WIDTH)
                for g in range(3)
            )
            both = jnp.concatenate([q, k], axis=0).astype(f32)
            both = both * lax.rsqrt(head_means(both * both, spread) + EPS)
            high, low = halves(both)
            goal = v.astype(f32) - both[BATCH * CH :]
            goal = goal - head_means(goal, spread)
            per_block = (BATCH, CH, WIDTH)
            xq[some, half] = both[: BATCH * CH].reshape(per_block)
            target[some, half] = goal.reshape(per_block)
            q_low[some, half] = high[: BATCH * CH].reshape(per_block)
            k_low[some, half] = high[BATCH * CH :].reshape(per_block)
            for h in heads:
                at = slice(h * HD, (h + 1) * HD)
                wide = jnp.concatenate([high[:, at], low[:, at], high[:, at]], axis=1)
                q_wide[h, some, half] = wide[: BATCH * CH].reshape(per_block)
                k_wide[h, some, half] = wide[BATCH * CH :].reshape(per_block)

    def project(h, state, bias, wide):
        high, low = halves(state)
        return dot(wide, jnp.concatenate([high, high, low], axis=0)) + bias

    for h in heads:
        at = slice(h * HD, (h + 1) * HD)
        start = weights[1, h].astype(f32)
        w2s[at, :] = start - jnp.mean(start, axis=0, keepdims=True)
        first = weights[0, h]
        w1s[at, :] = first.astype(f32)
        z1s[at, :] = dot(k_wide[h, 0, 0], jnp.concatenate([first, first, jnp.zeros_like(first)], axis=0))
    for ref in (b1s, b2s, q1s, a_prev, w2_prev, g2_prev, b2_prev):
        ref[...] = jnp.zeros_like(ref)

    gate = jnp.tanh(gate_ref[...])

    def query_first():
        high, low = halves(gelu_parts(q1s[...], False)[0])
        near = dot_nt(high, a_prev[...])
        deep = dot_nt(jnp.concatenate([high, low], axis=0), w2_prev[...])
        return near, deep, g2_prev[...], b2_prev[...]

    def query_last(state, source, half):
        near, deep, grad, bias = state
        near = jnp.where(causal, join_heads(near) + 1.0, 0.0).astype(bf16)
        out = join_heads(deep[:WIDTH] + deep[WIDTH:]) + bias - dot(near, grad)
        inner = xq[source, half] + out * lax.rsqrt(head_means(out * out, spread) + EPS)
        mixed[source, :, half * WIDTH : (half + 1) * WIDTH] = (attended[source, half] + gate * inner).astype(bf16)

    def one_block(now, later, before):
        z1, w1_now, w2_now, b1, b2 = z1s[...], w1s[...], w2s[...], b1s[...], b2s[...]
        goal = target[*now]
        query = query_first()

        keys = stack_heads(k_low[*now])
        cross = dot_nt(jnp.concatenate([q_low[*now], k_low[*later]], axis=0), keys) + 1.0
        cross = jnp.concatenate([jnp.where(causal, cross[:CH], 0.0), cross[CH:]], axis=0).astype(bf16)
        cross = stack_heads(cross)
        ahead = [
            project(
                h,
                w1_now[h * HD : (h + 1) * HD],
                b1[h],
                jnp.concatenate([q_wide[h, *now], k_wide[h, *later]], axis=0),
            )
            for h in heads
        ]

        act, slope = gelu_parts(z1, True)
        act_low = act.astype(bf16)
        w2_low = w2_now.astype(bf16)
        c = join_heads(dot_nt(act_low, w2_low)) + b2
        means = dot(jnp.concatenate([c * c, c * goal], axis=0).astype(bf16), spread)
        r = lax.rsqrt(means[:CH] + EPS)
        grad = (etas * r) * (c * (r * (EPS * r * r + means[CH:] * r)) - goal)
        grad_low = stack_heads(grad.astype(bf16))
        deep = dot(grad_low, w2_low) * slope
        deep_low = deep.astype(bf16)
        moved = dot(cross, deep_low)
        new_w2 = w2_now - dot_tn(grad_low, act_low)
        new_w1 = w1_now - dot_tn(keys, deep_low)
        new_b2 = b2 - jnp.sum(grad, axis=0, keepdims=True)
        new_b1 = [b1[h] - jnp.sum(deep[h * CH : (h + 1) * CH], axis=0, keepdims=True) for h in heads]
        query_last(query, *before)

        for h in heads:
            both = ahead[h] - moved[2 * h * CH : 2 * (h + 1) * CH]
            q1s[h * CH : (h + 1) * CH, :] = both[:CH]
            z1s[h * CH : (h + 1) * CH, :] = both[CH:]
            b1s[h] = new_b1[h]
        a_prev[...] = act_low
        w2_prev[...] = w2_low
        g2_prev[...] = grad_low
        b2_prev[...] = b2
        w1s[...] = new_w1
        w2s[...] = new_w2
        b2s[...] = new_b2

    def blocks(source, carry):
        last, ahead = jnp.maximum(source - 1, 0), jnp.minimum(source + 1, PARTS - 1)
        one_block((source, 0), (source, 1), (last, 1))
        one_block((source, 1), (ahead, 0), (source, 0))
        return carry

    lax.fori_loop(0, PARTS, blocks, 0, unroll=2)
    query_last(query_first(), PARTS - 1, 1)


VMEM = pl.BlockSpec(memory_space=pltpu.VMEM)
SMEM = pl.BlockSpec(memory_space=pltpu.SMEM)
HBM = pl.BlockSpec(memory_space=pltpu.HBM)


def run_heads(rate, pieces, seg, weights, gate):
    blocks = (PARTS, 2, CH, WIDTH)
    return pl.pallas_call(
        heads_kernel,
        out_shape=jax.ShapeDtypeStruct((PARTS, CH, 2 * WIDTH), bf16),
        in_specs=[SMEM] + [VMEM] * 4,
        out_specs=VMEM,
        scratch_shapes=[
            pltpu.VMEM(blocks, bf16),
            pltpu.VMEM(blocks, bf16),
            pltpu.VMEM((LOCAL,) + blocks, bf16),
            pltpu.VMEM((LOCAL,) + blocks, bf16),
            pltpu.VMEM(blocks, f32),
            pltpu.VMEM(blocks, f32),
            pltpu.VMEM(blocks, f32),
            pltpu.VMEM((WIDTH, FFI), f32),
            pltpu.VMEM((WIDTH, FFI), f32),
            pltpu.VMEM((LOCAL, 1, FFI), f32),
            pltpu.VMEM((1, WIDTH), f32),
            pltpu.VMEM((WIDTH, FFI), f32),
            pltpu.VMEM((WIDTH, FFI), f32),
            pltpu.VMEM((WIDTH, FFI), bf16),
            pltpu.VMEM((WIDTH, FFI), bf16),
            pltpu.VMEM((WIDTH, WIDTH), bf16),
            pltpu.VMEM((1, WIDTH), f32),
        ],
        compiler_params=pltpu.CompilerParams(vmem_limit_bytes=20 * MIB),
        cost_estimate=pl.CostEstimate(flops=4_000_000_000, bytes_accessed=100_000_000, transcendentals=0),
        name="run_heads",
    )(rate, pieces, seg, weights, gate)


STRIP = 512


def project_kernel(mixed, *rest):
    own, sib, out, groups, made, sems = rest[:4], rest[4:8], *rest[8:]
    core, dp = lax.rem(lax.axis_index("seq"), 2), lax.axis_index("dp")
    y, x = dp // 8, lax.rem(dp // 2, 4)
    for source in range(PARTS):
        for pair in range(2):
            for half in range(2):
                at = half * WIDTH + pair * 2 * ROWS
                groups[2 * source + pair, half * CH : (half + 1) * CH, :] = mixed[source, :, at : at + 2 * ROWS]
    copies = []
    for side, blocks in enumerate((own, sib)):
        axis = core if side == 0 else 1 - core
        left = []
        for far in STEPS:
            for near in STEPS:
                dx = jnp.where(axis == 0, near, far)
                dy = jnp.where(axis == 0, far, near)
                left.append(groups[lax.rem(y + 4 - dy, 4) * 4 + lax.rem(x + 4 - dx, 4)])
        left = jnp.concatenate(left, axis=1)
        wide = blocks[0].shape[1]
        for at in range(0, wide, STRIP):
            right = jnp.concatenate([block[:, at : at + STRIP] for block in blocks], axis=0)
            strip = slice(side * wide + at, side * wide + at + STRIP)
            made[:, strip] = dot(left, right).astype(bf16)
            to = pl.ds(pl.multiple_of(axis * wide + at, STRIP), STRIP)
            copies.append(pltpu.make_async_copy(made.at[:, strip], out.at[:, to], sems.at[len(copies)]))
            copies[-1].start()
    for copy in copies:
        copy.wait()


def run_project(mixed, own, sib):
    wide = own[0].shape[1]
    return pl.pallas_call(
        project_kernel,
        out_shape=jax.ShapeDtypeStruct((TOK, 2 * wide), bf16),
        in_specs=[VMEM] * 9,
        out_specs=HBM,
        scratch_shapes=[
            pltpu.VMEM((2 * PARTS, TOK, 2 * ROWS), bf16),
            pltpu.VMEM((TOK, 2 * wide), bf16),
            pltpu.SemaphoreType.DMA((2 * wide // STRIP,)),
        ],
        compiler_params=pltpu.CompilerParams(vmem_limit_bytes=16 * MIB),
        name="project_rows",
    )(mixed, *own, *sib)


ROWS = HH // 32
STEPS = (0, 1, 3, 2)


def where_is(index):
    dp, seq = divmod(index, PARTS)
    return dp // 8, (dp // 2) % 4, dp % 2, seq // 2, seq % 2


def index_of(y, x, z, group, core):
    return ((y % 4) * 8 + (x % 4) * 2 + z % 2) * PARTS + (group % 4) * 2 + core % 2


def move(array, place):
    pairs = [(i, index_of(*place(*where_is(i)))) for i in range(32 * PARTS)]
    return lax.ppermute(array, ("dp", "seq"), pairs)


def turn(array, step):
    return lax.ppermute(array, "seq", [(i, (i + step) % PARTS) for i in range(PARTS)])


def near_axis(step):
    return lambda y, x, z, group, core: (y + step * core, x + step * (1 - core), z, group, core)


def far_axis(step):
    return lambda y, x, z, group, core: (y + step * (1 - core), x + step * core, z, group, core)


def flip_z(y, x, z, group, core):
    return y, x, 1 - z, group, core


def flip_core(y, x, z, group, core):
    return y, x, z, group, 1 - core


def on_device(
    queries, key_states, value_states, segment_ids, inner_first, inner_second, inner_rate, branch_gate, out_weight
):
    seq, dp = lax.axis_index("seq"), lax.axis_index("dp")
    pieces, slab = pack(queries[0], key_states[0], value_states[0], out_weight)
    other = move(slab, flip_z)
    upper = dp % 2 == 1
    slab = jnp.concatenate([jnp.where(upper, other, slab), jnp.where(upper, slab, other)], axis=0)

    pieces = lax.all_to_all(pieces, "seq", split_axis=0, concat_axis=0, tiled=True)
    near = [move(slab, near_axis(step)) for step in STEPS[1:]]
    slab = jnp.concatenate([slab] + near, axis=0)
    own = [slab] + [move(slab, far_axis(step)) for step in STEPS[1:]]
    sib = [move(slab, flip_core)]

    weights = jnp.stack([lax.dynamic_slice_in_dim(w, seq * LOCAL, LOCAL, 0) for w in (inner_first, inner_second)])
    gate = lax.dynamic_slice_in_dim(branch_gate, seq * WIDTH, WIDTH, 0)[None]
    pieces, slab, gate, weights = lax.optimization_barrier((pieces, slab, gate, weights))
    mixed = run_heads(inner_rate, pieces, segment_ids, weights, gate)
    own = list(lax.optimization_barrier((tuple(own), mixed))[0])
    mixed = lax.all_to_all(mixed, "seq", split_axis=0, concat_axis=0, tiled=True)
    sib = [move(block, flip_core) for block in own]
    return run_project(mixed, own, sib)[None]


def solution(mesh):
    in_specs = (
        P("dp", "seq", None),
        P("dp", "seq", None),
        P("dp", "seq", None),
        P("dp", None),
        P(),
        P(),
        P(),
        P(),
        P("dp", None),
    )
    return jax.shard_map(
        on_device, mesh=mesh, in_specs=in_specs, out_specs=P("dp", "seq", None), check_vma=False
    )
```

```python
import functools
import math

import jax
import jax.numpy as jnp
from jax import lax
from jax.experimental import pallas as pl
from jax.experimental.pallas import tpu as pltpu
from jax.sharding import PartitionSpec as P

HD = 64
FFI = 256
CH = 64
BATCH = 4
LOCAL = 3
PARTS = 8
TOK = 128
LEN = 1024
HH = 1536
WIDTH = LOCAL * HD
SAME = 32.0
EPS = 1e-6
GA = math.sqrt(2.0 / math.pi)
GB = GA * 0.044715
MIB = 1024 * 1024

f32 = jnp.float32
bf16 = jnp.bfloat16


def dot(left, right):
    return jnp.dot(left, right, preferred_element_type=f32)


def dot_nt(left, right):
    return lax.dot_general(left, right, (((1,), (1,)), ((), ())), preferred_element_type=f32)


def dot_tn(left, right):
    return lax.dot_general(left, right, (((0,), (0,)), ((), ())), preferred_element_type=f32)


def lane_mean(value):
    return jnp.mean(value, axis=-1, keepdims=True)


def pack_kernel(q_ref, k_ref, v_ref, weight_ref, out, slab):
    wide = slab.shape[1]
    core = lax.rem(lax.axis_index("seq"), 2)
    slab[...] = weight_ref[:, pl.ds(pl.multiple_of(core * wide, wide), wide)]
    for part in range(PARTS):
        cols = slice(part * WIDTH, (part + 1) * WIDTH)
        for group, ref in enumerate((q_ref, k_ref, v_ref)):
            for half in range(2):
                at = (2 * group + half) * WIDTH
                out[part, :, at : at + WIDTH] = ref[half * CH : (half + 1) * CH, cols]


def pack(queries, keys, values, weight):
    return pl.pallas_call(
        pack_kernel,
        out_shape=[
            jax.ShapeDtypeStruct((PARTS, CH, 6 * WIDTH), bf16),
            jax.ShapeDtypeStruct((weight.shape[0], weight.shape[1] // 2), bf16),
        ],
        compiler_params=pltpu.CompilerParams(vmem_limit_bytes=62 * MIB),
        name="pack_rows",
    )(queries, keys, values, weight)


def gelu_parts(z, slope):
    square = z * z
    half = 0.5 * jnp.tanh(z * (GB * square + GA)) + 0.5
    act = z * half
    if not slope:
        return act, None
    return act, half + (act - act * half) * (6.0 * GB * square + 2.0 * GA)


def stack_heads(joint):
    head = lax.broadcasted_iota(jnp.int32, joint.shape, 1) // HD
    zero = jnp.zeros_like(joint)
    return jnp.concatenate([jnp.where(head == h, joint, zero) for h in range(LOCAL)], axis=0)


def join_heads(full):
    rows = full.shape[0] // LOCAL
    blocks = [full[h * rows : (h + 1) * rows] for h in range(LOCAL)]
    head = lax.broadcasted_iota(jnp.int32, blocks[0].shape, 1) // HD
    joint = blocks[0]
    for h in range(1, LOCAL):
        joint = jnp.where(head == h, blocks[h], joint)
    return joint


def halves(value):
    high = value.astype(bf16)
    return high, (value - high.astype(f32)).astype(bf16)


def head_means(value, spread):
    rows = value.shape[0]
    both = dot(jnp.concatenate(halves(value), axis=0), spread)
    return both[:rows] + both[rows:]


def heads_kernel(
    rate_ref, x, seg_ref, weights, gate_ref, mixed,
    q_low, k_low, q_wide, k_wide, xq, target, attended, w1s, w2s, b1s, b2s, z1s, q1s, a_prev,
    w2_prev, g2_prev, b2_prev, summed,
):
    me = lax.axis_index("seq")
    heads = range(LOCAL)
    column = lax.broadcasted_iota(jnp.int32, (WIDTH, WIDTH), 1) // HD
    row = lax.broadcasted_iota(jnp.int32, (WIDTH, WIDTH), 0) // HD
    spread = jnp.where(row == column, 1.0 / HD, 0.0).astype(bf16)
    token = lax.broadcasted_iota(jnp.int32, (CH, WIDTH), 0)
    causal = token >= lax.rem(lax.broadcasted_iota(jnp.int32, (CH, WIDTH), 1), HD)
    lane_head = lax.broadcasted_iota(jnp.int32, (1, WIDTH), 1) // HD
    etas = jnp.zeros((1, WIDTH), f32)
    for h in heads:
        etas = jnp.where(lane_head == h, rate_ref[me * LOCAL + h] * (1.0 / HD), etas)

    half_rows = PARTS * CH
    number = lax.broadcasted_iota(jnp.int32, (HD, LEN), 0)
    unit = jnp.where(
        lax.broadcasted_iota(jnp.int32, (HD, HD), 0) == lax.broadcasted_iota(jnp.int32, (HD, HD), 1), 1.0, 0.0
    )
    seg = dot_tn(jnp.where(seg_ref[...] == number, SAME, 0.0).astype(bf16), unit.astype(bf16)).astype(bf16)
    seg = seg.reshape(PARTS, 2, CH, HD)
    segs = [seg[:, half].reshape(half_rows, HD) for half in range(2)]

    def columns(group, h, half):
        at = (2 * group + half) * WIDTH + h * HD
        return x[:, :, at : at + HD].reshape(half_rows, HD)

    ones = jnp.ones((half_rows, HD), bf16)
    gathered = {}

    def attend(h, half):
        if h not in gathered:
            keys = [jnp.concatenate([columns(1, h, part), segs[part]], axis=1) for part in range(2)]
            values = [jnp.concatenate([columns(2, h, part), ones], axis=1) for part in range(2)]
            gathered[h] = jnp.concatenate(keys, axis=0), jnp.concatenate(values, axis=0)
        keys, values = gathered[h]
        q = jnp.concatenate([(columns(0, h, half) * 0.125).astype(bf16), segs[half]], axis=1)
        scores = dot_nt(q, keys)
        top = jnp.max(scores, axis=-1, keepdims=True)
        got = dot(jnp.exp(scores - top).astype(bf16), values)
        got = got[:, :HD] / got[:, HD:]
        attended[:, half, :, h * HD : (h + 1) * HD] = got.reshape(PARTS, CH, HD)

    def prepare(begin):
        some = slice(begin, begin + BATCH)
        for half in range(2):
            q, k, v = (
                x[some, :, (2 * g + half) * WIDTH : (2 * g + half + 1) * WIDTH].reshape(BATCH * CH, WIDTH)
                for g in range(3)
            )
            both = jnp.concatenate([q, k], axis=0).astype(f32)
            both = both * lax.rsqrt(head_means(both * both, spread) + EPS)
            high, low = halves(both)
            goal = v.astype(f32) - both[BATCH * CH :]
            goal = goal - head_means(goal, spread)
            per_block = (BATCH, CH, WIDTH)
            xq[some, half] = both[: BATCH * CH].reshape(per_block)
            target[some, half] = goal.reshape(per_block)
            q_low[some, half] = high[: BATCH * CH].reshape(per_block)
            k_low[some, half] = high[BATCH * CH :].reshape(per_block)
            for h in heads:
                at = slice(h * HD, (h + 1) * HD)
                wide = jnp.concatenate([high[:, at], low[:, at], high[:, at]], axis=1)
                q_wide[h, some, half] = wide[: BATCH * CH].reshape(per_block)
                k_wide[h, some, half] = wide[BATCH * CH :].reshape(per_block)

    prepare(0)

    def project(h, state, bias, wide):
        high, low = halves(state)
        return dot(wide, jnp.concatenate([high, high, low], axis=0)) + bias

    for h in heads:
        at = slice(h * HD, (h + 1) * HD)
        start = weights[1, h].astype(f32)
        w2s[at, :] = start - jnp.mean(start, axis=0, keepdims=True)
        first = weights[0, h]
        w1s[at, :] = first.astype(f32)
        z1s[at, :] = dot(k_wide[h, 0, 0], jnp.concatenate([first, first, jnp.zeros_like(first)], axis=0))
    for ref in (b1s, b2s, q1s, a_prev, w2_prev, g2_prev, b2_prev):
        ref[...] = jnp.zeros_like(ref)

    gate = jnp.tanh(gate_ref[...])

    def query_first():
        high, low = halves(gelu_parts(q1s[...], False)[0])
        near = dot_nt(high, a_prev[...])
        deep = dot_nt(jnp.concatenate([high, low], axis=0), w2_prev[...])
        return near, deep, g2_prev[...], b2_prev[...]

    def query_last(state, source, half):
        near, deep, grad, bias = state
        near = jnp.where(causal, join_heads(near) + 1.0, 0.0).astype(bf16)
        out = join_heads(deep[:WIDTH] + deep[WIDTH:]) + bias - dot(near, grad)
        inner = xq[source, half] + out * lax.rsqrt(head_means(out * out, spread) + EPS)
        summed[source, half] = gate * inner

    def one_block(now, later, before):
        z1, w1_now, w2_now, b1, b2 = z1s[...], w1s[...], w2s[...], b1s[...], b2s[...]
        goal = target[*now]
        query = query_first()

        keys = stack_heads(k_low[*now])
        cross = dot_nt(jnp.concatenate([q_low[*now], k_low[*later]], axis=0), keys) + 1.0
        cross = jnp.concatenate([jnp.where(causal, cross[:CH], 0.0), cross[CH:]], axis=0).astype(bf16)
        cross = stack_heads(cross)
        ahead = [
            project(
                h,
                w1_now[h * HD : (h + 1) * HD],
                b1[h],
                jnp.concatenate([q_wide[h, *now], k_wide[h, *later]], axis=0),
            )
            for h in heads
        ]

        act, slope = gelu_parts(z1, True)
        act_low = act.astype(bf16)
        w2_low = w2_now.astype(bf16)
        c = join_heads(dot_nt(act_low, w2_low)) + b2
        means = dot(jnp.concatenate([c * c, c * goal], axis=0).astype(bf16), spread)
        r = lax.rsqrt(means[:CH] + EPS)
        grad = (etas * r) * (c * (r * (EPS * r * r + means[CH:] * r)) - goal)
        grad_low = stack_heads(grad.astype(bf16))
        deep = dot(grad_low, w2_low) * slope
        deep_low = deep.astype(bf16)
        moved = dot(cross, deep_low)
        new_w2 = w2_now - dot_tn(grad_low, act_low)
        new_w1 = w1_now - dot_tn(keys, deep_low)
        new_b2 = b2 - jnp.sum(grad, axis=0, keepdims=True)
        new_b1 = [b1[h] - jnp.sum(deep[h * CH : (h + 1) * CH], axis=0, keepdims=True) for h in heads]
        query_last(query, *before)

        for h in heads:
            both = ahead[h] - moved[2 * h * CH : 2 * (h + 1) * CH]
            q1s[h * CH : (h + 1) * CH, :] = both[:CH]
            z1s[h * CH : (h + 1) * CH, :] = both[CH:]
            b1s[h] = new_b1[h]
        a_prev[...] = act_low
        w2_prev[...] = w2_low
        g2_prev[...] = grad_low
        b2_prev[...] = b2
        w1s[...] = new_w1
        w2s[...] = new_w2
        b2s[...] = new_b2

    units = [(h, half) for h in heads for half in range(2)]
    for source in range(PARTS):
        last, ahead = max(source - 1, 0), min(source + 1, PARTS - 1)
        one_block((source, 0), (source, 1), (last, 1))
        if ahead % BATCH == 0 and ahead > source:
            prepare(ahead)
        one_block((source, 1), (ahead, 0), (source, 0))
        if source < len(units):
            attend(*units[source])
    query_last(query_first(), PARTS - 1, 1)
    for half in range(2):
        mixed[:, :, half * WIDTH : (half + 1) * WIDTH] = (attended[:, half] + summed[:, half]).astype(bf16)


VMEM = pl.BlockSpec(memory_space=pltpu.VMEM)
SMEM = pl.BlockSpec(memory_space=pltpu.SMEM)
HBM = pl.BlockSpec(memory_space=pltpu.HBM)


def run_heads(rate, pieces, seg, weights, gate):
    blocks = (PARTS, 2, CH, WIDTH)
    return pl.pallas_call(
        heads_kernel,
        out_shape=jax.ShapeDtypeStruct((PARTS, CH, 2 * WIDTH), bf16),
        in_specs=[SMEM] + [VMEM] * 4,
        out_specs=VMEM,
        scratch_shapes=[
            pltpu.VMEM(blocks, bf16),
            pltpu.VMEM(blocks, bf16),
            pltpu.VMEM((LOCAL,) + blocks, bf16),
            pltpu.VMEM((LOCAL,) + blocks, bf16),
            pltpu.VMEM(blocks, f32),
            pltpu.VMEM(blocks, f32),
            pltpu.VMEM(blocks, f32),
            pltpu.VMEM((WIDTH, FFI), f32),
            pltpu.VMEM((WIDTH, FFI), f32),
            pltpu.VMEM((LOCAL, 1, FFI), f32),
            pltpu.VMEM((1, WIDTH), f32),
            pltpu.VMEM((WIDTH, FFI), f32),
            pltpu.VMEM((WIDTH, FFI), f32),
            pltpu.VMEM((WIDTH, FFI), bf16),
            pltpu.VMEM((WIDTH, FFI), bf16),
            pltpu.VMEM((WIDTH, WIDTH), bf16),
            pltpu.VMEM((1, WIDTH), f32),
            pltpu.VMEM(blocks, f32),
        ],
        compiler_params=pltpu.CompilerParams(vmem_limit_bytes=20 * MIB),
        cost_estimate=pl.CostEstimate(flops=4_000_000_000, bytes_accessed=100_000_000, transcendentals=0),
        name="run_heads",
    )(rate, pieces, seg, weights, gate)


STRIP = 512


def project_kernel(mixed, *rest):
    own, sib, out, groups, made, sems = rest[:4], rest[4:8], *rest[8:]
    core, dp = lax.rem(lax.axis_index("seq"), 2), lax.axis_index("dp")
    y, x = dp // 8, lax.rem(dp // 2, 4)
    for source in range(PARTS):
        for pair in range(2):
            for half in range(2):
                at = half * WIDTH + pair * 2 * ROWS
                groups[2 * source + pair, half * CH : (half + 1) * CH, :] = mixed[source, :, at : at + 2 * ROWS]
    copies = []
    for side, blocks in enumerate((own, sib)):
        axis = core if side == 0 else 1 - core
        left = []
        for far in STEPS:
            for near in STEPS:
                dx = jnp.where(axis == 0, near, far)
                dy = jnp.where(axis == 0, far, near)
                left.append(groups[lax.rem(y + 4 - dy, 4) * 4 + lax.rem(x + 4 - dx, 4)])
        left = jnp.concatenate(left, axis=1)
        wide = blocks[0].shape[1]
        for at in range(0, wide, STRIP):
            right = jnp.concatenate([block[:, at : at + STRIP] for block in blocks], axis=0)
            strip = slice(side * wide + at, side * wide + at + STRIP)
            made[:, strip] = dot(left, right).astype(bf16)
            to = pl.ds(pl.multiple_of(axis * wide + at, STRIP), STRIP)
            copies.append(pltpu.make_async_copy(made.at[:, strip], out.at[:, to], sems.at[len(copies)]))
            copies[-1].start()
    for copy in copies:
        copy.wait()


def run_project(mixed, own, sib):
    wide = own[0].shape[1]
    return pl.pallas_call(
        project_kernel,
        out_shape=jax.ShapeDtypeStruct((TOK, 2 * wide), bf16),
        in_specs=[VMEM] * 9,
        out_specs=HBM,
        scratch_shapes=[
            pltpu.VMEM((2 * PARTS, TOK, 2 * ROWS), bf16),
            pltpu.VMEM((TOK, 2 * wide), bf16),
            pltpu.SemaphoreType.DMA((2 * wide // STRIP,)),
        ],
        compiler_params=pltpu.CompilerParams(vmem_limit_bytes=16 * MIB),
        name="project_rows",
    )(mixed, *own, *sib)


ROWS = HH // 32
STEPS = (0, 1, 3, 2)


def where_is(index):
    dp, seq = divmod(index, PARTS)
    return dp // 8, (dp // 2) % 4, dp % 2, seq // 2, seq % 2


def index_of(y, x, z, group, core):
    return ((y % 4) * 8 + (x % 4) * 2 + z % 2) * PARTS + (group % 4) * 2 + core % 2


def move(array, place):
    pairs = [(i, index_of(*place(*where_is(i)))) for i in range(32 * PARTS)]
    return lax.ppermute(array, ("dp", "seq"), pairs)


def turn(array, step):
    return lax.ppermute(array, "seq", [(i, (i + step) % PARTS) for i in range(PARTS)])


def near_axis(step):
    return lambda y, x, z, group, core: (y + step * core, x + step * (1 - core), z, group, core)


def far_axis(step):
    return lambda y, x, z, group, core: (y + step * (1 - core), x + step * core, z, group, core)


def flip_z(y, x, z, group, core):
    return y, x, 1 - z, group, core


def flip_core(y, x, z, group, core):
    return y, x, z, group, 1 - core


def on_device(
    queries, key_states, value_states, segment_ids, inner_first, inner_second, inner_rate, branch_gate, out_weight
):
    seq, dp = lax.axis_index("seq"), lax.axis_index("dp")
    pieces, slab = pack(queries[0], key_states[0], value_states[0], out_weight)
    other = move(slab, flip_z)
    upper = dp % 2 == 1
    slab = jnp.concatenate([jnp.where(upper, other, slab), jnp.where(upper, slab, other)], axis=0)

    pieces = lax.all_to_all(pieces, "seq", split_axis=0, concat_axis=0, tiled=True)
    near = [move(slab, near_axis(step)) for step in STEPS[1:]]
    slab = jnp.concatenate([slab] + near, axis=0)
    own = [slab] + [move(slab, far_axis(step)) for step in STEPS[1:]]
    sib = [move(slab, flip_core)]

    weights = jnp.stack([lax.dynamic_slice_in_dim(w, seq * LOCAL, LOCAL, 0) for w in (inner_first, inner_second)])
    gate = lax.dynamic_slice_in_dim(branch_gate, seq * WIDTH, WIDTH, 0)[None]
    pieces, slab, gate, weights = lax.optimization_barrier((pieces, slab, gate, weights))
    mixed = run_heads(inner_rate, pieces, segment_ids, weights, gate)
    own = list(lax.optimization_barrier((tuple(own), mixed))[0])
    mixed = lax.all_to_all(mixed, "seq", split_axis=0, concat_axis=0, tiled=True)
    sib = [move(block, flip_core) for block in own]
    return run_project(mixed, own, sib)[None]


def solution(mesh):
    in_specs = (
        P("dp", "seq", None),
        P("dp", "seq", None),
        P("dp", "seq", None),
        P("dp", None),
        P(),
        P(),
        P(),
        P(),
        P("dp", None),
    )
    return jax.shard_map(
        on_device, mesh=mesh, in_specs=in_specs, out_specs=P("dp", "seq", None), check_vma=False
    )
```

```python
import functools
import math

import jax
import jax.numpy as jnp
from jax import lax
from jax.experimental import pallas as pl
from jax.experimental.pallas import tpu as pltpu
from jax.sharding import PartitionSpec as P

HD = 64
FFI = 256
CH = 64
BATCH = 4
LOCAL = 3
PARTS = 8
TOK = 128
LEN = 1024
HH = 1536
WIDTH = LOCAL * HD
SAME = 32.0
EPS = 1e-6
GA = math.sqrt(2.0 / math.pi)
GB = GA * 0.044715
MIB = 1024 * 1024

f32 = jnp.float32
bf16 = jnp.bfloat16


def dot(left, right):
    return jnp.dot(left, right, preferred_element_type=f32)


def dot_nt(left, right):
    return lax.dot_general(left, right, (((1,), (1,)), ((), ())), preferred_element_type=f32)


def dot_tn(left, right):
    return lax.dot_general(left, right, (((0,), (0,)), ((), ())), preferred_element_type=f32)


def lane_mean(value):
    return jnp.mean(value, axis=-1, keepdims=True)


def pack_kernel(q_ref, k_ref, v_ref, weight_ref, out, slab):
    wide = slab.shape[1]
    core = lax.rem(lax.axis_index("seq"), 2)
    slab[...] = weight_ref[:, pl.ds(pl.multiple_of(core * wide, wide), wide)]
    for part in range(PARTS):
        cols = slice(part * WIDTH, (part + 1) * WIDTH)
        for group, ref in enumerate((q_ref, k_ref, v_ref)):
            for half in range(2):
                at = (2 * group + half) * WIDTH
                out[part, :, at : at + WIDTH] = ref[half * CH : (half + 1) * CH, cols]


def pack(queries, keys, values, weight):
    return pl.pallas_call(
        pack_kernel,
        out_shape=[
            jax.ShapeDtypeStruct((PARTS, CH, 6 * WIDTH), bf16),
            jax.ShapeDtypeStruct((weight.shape[0], weight.shape[1] // 2), bf16),
        ],
        compiler_params=pltpu.CompilerParams(vmem_limit_bytes=62 * MIB),
        name="pack_rows",
    )(queries, keys, values, weight)


def gelu_parts(z, slope):
    square = z * z
    half = 0.5 * jnp.tanh(z * (GB * square + GA)) + 0.5
    act = z * half
    if not slope:
        return act, None
    return act, half + (act - act * half) * (6.0 * GB * square + 2.0 * GA)


def stack_heads(joint):
    head = lax.broadcasted_iota(jnp.int32, joint.shape, 1) // HD
    zero = jnp.zeros_like(joint)
    return jnp.concatenate([jnp.where(head == h, joint, zero) for h in range(LOCAL)], axis=0)


def join_heads(full):
    rows = full.shape[0] // LOCAL
    blocks = [full[h * rows : (h + 1) * rows] for h in range(LOCAL)]
    head = lax.broadcasted_iota(jnp.int32, blocks[0].shape, 1) // HD
    joint = blocks[0]
    for h in range(1, LOCAL):
        joint = jnp.where(head == h, blocks[h], joint)
    return joint


def halves(value):
    high = value.astype(bf16)
    return high, (value - high.astype(f32)).astype(bf16)


def head_means(value, spread):
    rows = value.shape[0]
    both = dot(jnp.concatenate(halves(value), axis=0), spread)
    return both[:rows] + both[rows:]


def heads_kernel(
    rate_ref, x, seg_ref, weights, gate_ref, mixed,
    q_low, k_low, q_wide, k_wide, xq, target, attended, summed,
):
    me = lax.axis_index("seq")
    heads = range(LOCAL)
    column = lax.broadcasted_iota(jnp.int32, (WIDTH, WIDTH), 1) // HD
    row = lax.broadcasted_iota(jnp.int32, (WIDTH, WIDTH), 0) // HD
    spread = jnp.where(row == column, 1.0 / HD, 0.0).astype(bf16)
    token = lax.broadcasted_iota(jnp.int32, (CH, WIDTH), 0)
    causal = token >= lax.rem(lax.broadcasted_iota(jnp.int32, (CH, WIDTH), 1), HD)
    lane_head = lax.broadcasted_iota(jnp.int32, (1, WIDTH), 1) // HD
    etas = jnp.zeros((1, WIDTH), f32)
    for h in heads:
        etas = jnp.where(lane_head == h, rate_ref[me * LOCAL + h] * (1.0 / HD), etas)

    half_rows = PARTS * CH
    number = lax.broadcasted_iota(jnp.int32, (HD, LEN), 0)
    unit = jnp.where(
        lax.broadcasted_iota(jnp.int32, (HD, HD), 0) == lax.broadcasted_iota(jnp.int32, (HD, HD), 1), 1.0, 0.0
    )
    seg = dot_tn(jnp.where(seg_ref[...] == number, SAME, 0.0).astype(bf16), unit.astype(bf16)).astype(bf16)
    seg = seg.reshape(PARTS, 2, CH, HD)
    segs = [seg[:, half].reshape(half_rows, HD) for half in range(2)]

    def columns(group, h, half):
        at = (2 * group + half) * WIDTH + h * HD
        return x[:, :, at : at + HD].reshape(half_rows, HD)

    ones = jnp.ones((half_rows, HD), bf16)
    gathered = {}

    def attend(h, half):
        if h not in gathered:
            keys = [jnp.concatenate([columns(1, h, part), segs[part]], axis=1) for part in range(2)]
            values = [jnp.concatenate([columns(2, h, part), ones], axis=1) for part in range(2)]
            gathered[h] = jnp.concatenate(keys, axis=0), jnp.concatenate(values, axis=0)
        keys, values = gathered[h]
        q = jnp.concatenate([(columns(0, h, half) * 0.125).astype(bf16), segs[half]], axis=1)
        scores = dot_nt(q, keys)
        top = jnp.max(scores, axis=-1, keepdims=True)
        got = dot(jnp.exp(scores - top).astype(bf16), values)
        got = got[:, :HD] / got[:, HD:]
        attended[:, half, :, h * HD : (h + 1) * HD] = got.reshape(PARTS, CH, HD)

    def prepare(begin):
        some = slice(begin, begin + BATCH)
        for half in range(2):
            q, k, v = (
                x[some, :, (2 * g + half) * WIDTH : (2 * g + half + 1) * WIDTH].reshape(BATCH * CH, WIDTH)
                for g in range(3)
            )
            both = jnp.concatenate([q, k], axis=0).astype(f32)
            both = both * lax.rsqrt(head_means(both * both, spread) + EPS)
            high, low = halves(both)
            goal = v.astype(f32) - both[BATCH * CH :]
            goal = goal - head_means(goal, spread)
            per_block = (BATCH, CH, WIDTH)
            xq[some, half] = both[: BATCH * CH].reshape(per_block)
            target[some, half] = goal.reshape(per_block)
            q_low[some, half] = high[: BATCH * CH].reshape(per_block)
            k_low[some, half] = high[BATCH * CH :].reshape(per_block)
            for h in heads:
                at = slice(h * HD, (h + 1) * HD)
                wide = jnp.concatenate([high[:, at], low[:, at], high[:, at]], axis=1)
                q_wide[h, some, half] = wide[: BATCH * CH].reshape(per_block)
                k_wide[h, some, half] = wide[BATCH * CH :].reshape(per_block)

    prepare(0)

    def project(h, state, bias, wide):
        high, low = halves(state)
        return dot(wide, jnp.concatenate([high, high, low], axis=0)) + bias

    starts = [weights[1, h].astype(f32) for h in heads]
    firsts = [weights[0, h] for h in heads]
    state = (
        jnp.concatenate(
            [
                dot(k_wide[h, 0, 0], jnp.concatenate([firsts[h], firsts[h], jnp.zeros_like(firsts[h])], axis=0))
                for h in heads
            ],
            axis=0,
        ),
        jnp.concatenate(firsts, axis=0).astype(f32),
        jnp.concatenate([start - jnp.mean(start, axis=0, keepdims=True) for start in starts], axis=0),
        [jnp.zeros((1, FFI), f32) for h in heads],
        jnp.zeros((1, WIDTH), f32),
    )

    gate = jnp.tanh(gate_ref[...])

    def query_first(q1, act_low, w2_low, grad_low, bias):
        high, low = halves(gelu_parts(q1, False)[0])
        near = dot_nt(high, act_low)
        deep = dot_nt(jnp.concatenate([high, low], axis=0), w2_low)
        return near, deep, grad_low, bias

    def query_last(state, source, half):
        near, deep, grad, bias = state
        near = jnp.where(causal, join_heads(near) + 1.0, 0.0).astype(bf16)
        out = join_heads(deep[:WIDTH] + deep[WIDTH:]) + bias - dot(near, grad)
        inner = xq[source, half] + out * lax.rsqrt(head_means(out * out, spread) + EPS)
        summed[source, half] = gate * inner

    def one_block(state, held, now, later, before):
        z1, w1_now, w2_now, b1, b2 = state
        goal = target[*now]
        query = query_first(*held) if held else None

        keys = stack_heads(k_low[*now])
        cross = dot_nt(jnp.concatenate([q_low[*now], k_low[*later]], axis=0), keys) + 1.0
        cross = jnp.concatenate([jnp.where(causal, cross[:CH], 0.0), cross[CH:]], axis=0).astype(bf16)
        cross = stack_heads(cross)
        ahead = [
            project(
                h,
                w1_now[h * HD : (h + 1) * HD],
                b1[h],
                jnp.concatenate([q_wide[h, *now], k_wide[h, *later]], axis=0),
            )
            for h in heads
        ]

        act, slope = gelu_parts(z1, True)
        act_low = act.astype(bf16)
        w2_low = w2_now.astype(bf16)
        c = join_heads(dot_nt(act_low, w2_low)) + b2
        means = dot(jnp.concatenate([c * c, c * goal], axis=0).astype(bf16), spread)
        r = lax.rsqrt(means[:CH] + EPS)
        grad = (etas * r) * (c * (r * (EPS * r * r + means[CH:] * r)) - goal)
        grad_low = stack_heads(grad.astype(bf16))
        deep = dot(grad_low, w2_low) * slope
        deep_low = deep.astype(bf16)
        moved = dot(cross, deep_low)
        new_w2 = w2_now - dot_tn(grad_low, act_low)
        new_w1 = w1_now - dot_tn(keys, deep_low)
        new_b2 = b2 - jnp.sum(grad, axis=0, keepdims=True)
        new_b1 = [b1[h] - jnp.sum(deep[h * CH : (h + 1) * CH], axis=0, keepdims=True) for h in heads]
        if held:
            query_last(query, *before)

        both = [ahead[h] - moved[2 * h * CH : 2 * (h + 1) * CH] for h in heads]
        q1 = jnp.concatenate([rows[:CH] for rows in both], axis=0)
        z1 = jnp.concatenate([rows[CH:] for rows in both], axis=0)
        return (z1, new_w1, new_w2, new_b1, new_b2), (q1, act_low, w2_low, grad_low, b2)

    units = [(h, half) for h in heads for half in range(2)]
    held = None
    for source in range(PARTS):
        last, ahead = max(source - 1, 0), min(source + 1, PARTS - 1)
        state, held = one_block(state, held, (source, 0), (source, 1), (last, 1))
        if ahead % BATCH == 0 and ahead > source:
            prepare(ahead)
        state, held = one_block(state, held, (source, 1), (ahead, 0), (source, 0))
        if source < len(units):
            attend(*units[source])
    query_last(query_first(*held), PARTS - 1, 1)
    for half in range(2):
        mixed[:, :, half * WIDTH : (half + 1) * WIDTH] = (attended[:, half] + summed[:, half]).astype(bf16)


VMEM = pl.BlockSpec(memory_space=pltpu.VMEM)
SMEM = pl.BlockSpec(memory_space=pltpu.SMEM)
HBM = pl.BlockSpec(memory_space=pltpu.HBM)


def run_heads(rate, pieces, seg, weights, gate):
    blocks = (PARTS, 2, CH, WIDTH)
    return pl.pallas_call(
        heads_kernel,
        out_shape=jax.ShapeDtypeStruct((PARTS, CH, 2 * WIDTH), bf16),
        in_specs=[SMEM] + [VMEM] * 4,
        out_specs=VMEM,
        scratch_shapes=[
            pltpu.VMEM(blocks, bf16),
            pltpu.VMEM(blocks, bf16),
            pltpu.VMEM((LOCAL,) + blocks, bf16),
            pltpu.VMEM((LOCAL,) + blocks, bf16),
            pltpu.VMEM(blocks, f32),
            pltpu.VMEM(blocks, f32),
            pltpu.VMEM(blocks, f32),
            pltpu.VMEM(blocks, f32),
        ],
        compiler_params=pltpu.CompilerParams(vmem_limit_bytes=20 * MIB),
        cost_estimate=pl.CostEstimate(flops=4_000_000_000, bytes_accessed=100_000_000, transcendentals=0),
        name="run_heads",
    )(rate, pieces, seg, weights, gate)


STRIP = 512


def project_kernel(mixed, *rest):
    own, sib, out, groups, made, sems = rest[:4], rest[4:8], *rest[8:]
    core, dp = lax.rem(lax.axis_index("seq"), 2), lax.axis_index("dp")
    y, x = dp // 8, lax.rem(dp // 2, 4)
    for source in range(PARTS):
        for pair in range(2):
            for half in range(2):
                at = half * WIDTH + pair * 2 * ROWS
                groups[2 * source + pair, half * CH : (half + 1) * CH, :] = mixed[source, :, at : at + 2 * ROWS]
    copies = []
    for side, blocks in enumerate((own, sib)):
        axis = core if side == 0 else 1 - core
        left = []
        for far in STEPS:
            for near in STEPS:
                dx = jnp.where(axis == 0, near, far)
                dy = jnp.where(axis == 0, far, near)
                left.append(groups[lax.rem(y + 4 - dy, 4) * 4 + lax.rem(x + 4 - dx, 4)])
        left = jnp.concatenate(left, axis=1)
        wide = blocks[0].shape[1]
        for at in range(0, wide, STRIP):
            right = jnp.concatenate([block[:, at : at + STRIP] for block in blocks], axis=0)
            strip = slice(side * wide + at, side * wide + at + STRIP)
            made[:, strip] = dot(left, right).astype(bf16)
            to = pl.ds(pl.multiple_of(axis * wide + at, STRIP), STRIP)
            copies.append(pltpu.make_async_copy(made.at[:, strip], out.at[:, to], sems.at[len(copies)]))
            copies[-1].start()
    for copy in copies:
        copy.wait()


def run_project(mixed, own, sib):
    wide = own[0].shape[1]
    return pl.pallas_call(
        project_kernel,
        out_shape=jax.ShapeDtypeStruct((TOK, 2 * wide), bf16),
        in_specs=[VMEM] * 9,
        out_specs=HBM,
        scratch_shapes=[
            pltpu.VMEM((2 * PARTS, TOK, 2 * ROWS), bf16),
            pltpu.VMEM((TOK, 2 * wide), bf16),
            pltpu.SemaphoreType.DMA((2 * wide // STRIP,)),
        ],
        compiler_params=pltpu.CompilerParams(vmem_limit_bytes=16 * MIB),
        name="project_rows",
    )(mixed, *own, *sib)


ROWS = HH // 32
STEPS = (0, 1, 3, 2)


def where_is(index):
    dp, seq = divmod(index, PARTS)
    return dp // 8, (dp // 2) % 4, dp % 2, seq // 2, seq % 2


def index_of(y, x, z, group, core):
    return ((y % 4) * 8 + (x % 4) * 2 + z % 2) * PARTS + (group % 4) * 2 + core % 2


def move(array, place):
    pairs = [(i, index_of(*place(*where_is(i)))) for i in range(32 * PARTS)]
    return lax.ppermute(array, ("dp", "seq"), pairs)


def turn(array, step):
    return lax.ppermute(array, "seq", [(i, (i + step) % PARTS) for i in range(PARTS)])


def near_axis(step):
    return lambda y, x, z, group, core: (y + step * core, x + step * (1 - core), z, group, core)


def far_axis(step):
    return lambda y, x, z, group, core: (y + step * (1 - core), x + step * core, z, group, core)


def flip_z(y, x, z, group, core):
    return y, x, 1 - z, group, core


def flip_core(y, x, z, group, core):
    return y, x, z, group, 1 - core


def on_device(
    queries, key_states, value_states, segment_ids, inner_first, inner_second, inner_rate, branch_gate, out_weight
):
    seq, dp = lax.axis_index("seq"), lax.axis_index("dp")
    pieces, slab = pack(queries[0], key_states[0], value_states[0], out_weight)
    other = move(slab, flip_z)
    upper = dp % 2 == 1
    slab = jnp.concatenate([jnp.where(upper, other, slab), jnp.where(upper, slab, other)], axis=0)

    pieces = lax.all_to_all(pieces, "seq", split_axis=0, concat_axis=0, tiled=True)
    near = [move(slab, near_axis(step)) for step in STEPS[1:]]
    slab = jnp.concatenate([slab] + near, axis=0)
    own = [slab] + [move(slab, far_axis(step)) for step in STEPS[1:]]
    sib = [move(slab, flip_core)]

    weights = jnp.stack([lax.dynamic_slice_in_dim(w, seq * LOCAL, LOCAL, 0) for w in (inner_first, inner_second)])
    gate = lax.dynamic_slice_in_dim(branch_gate, seq * WIDTH, WIDTH, 0)[None]
    pieces, slab, gate, weights = lax.optimization_barrier((pieces, slab, gate, weights))
    mixed = run_heads(inner_rate, pieces, segment_ids, weights, gate)
    own = list(lax.optimization_barrier((tuple(own), mixed))[0])
    mixed = lax.all_to_all(mixed, "seq", split_axis=0, concat_axis=0, tiled=True)
    sib = [move(block, flip_core) for block in own]
    return run_project(mixed, own, sib)[None]


def solution(mesh):
    in_specs = (
        P("dp", "seq", None),
        P("dp", "seq", None),
        P("dp", "seq", None),
        P("dp", None),
        P(),
        P(),
        P(),
        P(),
        P("dp", None),
    )
    return jax.shard_map(
        on_device, mesh=mesh, in_specs=in_specs, out_specs=P("dp", "seq", None), check_vma=False
    )
```
